32 devices in a mesh: dp: 8 (over z, x), mp: 4 (over y, core).
Axes of the slice: x: 2, y: 2, z: 4, core: 2. Of those that a mesh axis runs over, the one named last changes fastest.
Arguments:
- new_rows: bfloat16 [256, 8, 4, 1536], P(None, 'dp', None, 'mp'), may hold values from -50 to 50
- counts: int32 [8], replicated, may hold values from 1 to 640, 2048 in all
- history_len: int32 [8], replicated, may hold values from 1 to 512, as said below
- user_owner: int32 [8], replicated, may hold values from 0 to 7, each once
- cache_kv: bfloat16 [8, 512, 2, 1536], P('dp', None, None, 'mp'), may hold values from -50 to 50
- w_out: bfloat16 [1536, 1536], P(None, 'mp'), may hold values from -0.15625 to 0.15625
Outputs:
- new_kv: bfloat16 [8, 640, 2, 1536], P('dp', None, None, 'mp')
- layer_out: bfloat16 [8, 640, 1536], P('dp', None, 'mp')
The draws below stay inside these ranges and needn't reach their ends.
Inputs may be any that keep to these rules, and one draw needn't show every extreme that they name: `counts`: each user has at least one new event, 2048 in all; some user has exactly 640. `history_len`: some user has exactly 512. `user_owner`: A permutation of the cache slots.
All inputs are finite; a program needn't handle non-finite values.
Results may differ from the reference program's by a relative error of at most 0.0057.
Values may be sent and summed in bfloat16 or wider, within the bound.
A program may use at most 64 MiB of HBM per device.

```python
import math
import jax
import jax.numpy as jnp
import numpy as np
from jax import lax

D = 1536
H = 12
DH = 128
HD = 1536
ROWS_DEV = 256
HIST = 512
CAP = 640
USERS = 8
ROWS = 2048


def head_scales(key):
    spread = math.log(10.0)
    return jnp.exp(jax.random.uniform(jax.random.fold_in(key, 11), (H,), jnp.float32, 0.0, spread))


def base_values(key, shape):
    drawn = jnp.clip(jax.random.normal(key, shape, jnp.float32), -5.0, 5.0)
    return drawn


def draw_new_rows(key, part):
    drawn = base_values(jax.random.fold_in(key, 3), (ROWS_DEV, USERS, 4, H, DH))
    factor = jnp.ones((4, H), jnp.float32).at[2].set(head_scales(key))
    return (drawn * factor[None, None, :, :, None]).reshape(ROWS_DEV, USERS, 4, H * DH).astype(jnp.bfloat16)


def draw_cache_kv(key, part):
    drawn = base_values(jax.random.fold_in(key, 5), (USERS, HIST, 2, H, DH))
    factor = jnp.ones((2, H), jnp.float32).at[1].set(head_scales(key))
    return (drawn * factor[None, None, :, :, None]).reshape(USERS, HIST, 2, H * DH).astype(jnp.bfloat16)


def draw_history_len(key, part):
    lengths = jax.random.randint(jax.random.fold_in(key, 7), (USERS,), 1, HIST + 1, jnp.int32)
    chosen = jax.random.randint(jax.random.fold_in(key, 9), (), 0, USERS, jnp.int32)
    return lengths.at[chosen].set(HIST)


def levels(own_key, dims, cuts, low, top_value):
    factor_of = 1.0
    for axis_at, parts in cuts:
        draws = jax.random.uniform(jax.random.fold_in(jax.random.fold_in(own_key, 6), axis_at), (parts,), jnp.float32, low / len(cuts), top_value / len(cuts))
        factor_of = factor_of * jnp.repeat(jnp.exp(draws), dims[axis_at] // parts).reshape((-1,) + (1,) * (len(dims) - 1 - axis_at))
    return factor_of


def split_up(amount, total, reach, skew):
    loads = [(1 << 20) // math.isqrt(grade ** skew) + 1 for grade in range(2, amount + 1)]
    spare, holding = total - reach - (amount - 1), [1] * (amount - 1)
    while spare > 0:
        movable = [i for i in range(amount - 1) if holding[i] < reach]
        mass, budget = sum([loads[i] for i in movable]), spare
        for i in movable:
            addition = min(reach - holding[i], max(1, budget * loads[i] // mass), spare)
            holding[i] = holding[i] + addition
            spare = spare - addition
    return np.array([reach] + holding)


def uneven(stream_key, number_of, total, reach, skew):
    if number_of == 2:
        one = jax.random.randint(stream_key, (), max(1, total - reach), min(reach, total - 1) + 1)
        return jnp.stack([one, total - one])
    sizes = jnp.asarray(split_up(number_of, total, reach, skew), jnp.int32)
    pairs = (number_of - 1) // 2
    donor, taker = sizes[1:1 + 2 * pairs:2], sizes[2:2 + 2 * pairs:2]
    slack = jnp.minimum(donor - 1, reach - taker)
    passed = jax.random.randint(jax.random.fold_in(stream_key, 1), (pairs,), 0, 1 << 20) % (slack + 1)
    sizes = sizes.at[1:1 + 2 * pairs:2].set(donor - passed).at[2:2 + 2 * pairs:2].set(taker + passed)
    return sizes[jax.random.permutation(jax.random.fold_in(stream_key, 2), number_of)]


def scatter_about(key, shape, deviation, limit, cuts=(), held_as=jnp.bfloat16):
    array = deviation * jax.random.normal(key, shape, jnp.float32)
    if cuts:
        array = array * levels(key, shape, cuts, -0.22, 0.18)
    return jnp.clip(array, -limit, limit).astype(held_as)


def setup_inputs(seed: int = 0) -> dict:
    splits = jax.random.split(jax.random.key(seed), 7)
    new_rows = draw_new_rows(jax.random.fold_in(splits[6], 71), 0)
    counts = uneven(splits[1], USERS, ROWS, CAP, 2).astype(jnp.int32)
    history_len = draw_history_len(jax.random.fold_in(splits[6], 71), 0)
    user_owner = jax.random.permutation(splits[3], USERS).astype(jnp.int32)
    cache_kv = draw_cache_kv(jax.random.fold_in(splits[6], 71), 0)
    w_out = scatter_about(splits[5], (HD, D), HD ** -0.5, 0.15625, ((1, 4),))
    return dict(new_rows=new_rows, counts=counts, history_len=history_len, user_owner=user_owner, cache_kv=cache_kv, w_out=w_out)


EPSILON = 1e-06

def reference(new_rows, counts, history_len, user_owner, cache_kv, w_out):
    events = new_rows.reshape(ROWS, 4, HD)
    starts = (jnp.cumsum(counts) - counts).astype(jnp.int32)
    positions = jnp.arange(CAP, dtype=jnp.int32)
    score_scale = 1.0 / DH ** 0.5

    def per_owner(slot_index):
        is_mine = (user_owner == slot_index).astype(jnp.int32)
        new_count = jnp.sum(counts * is_mine).astype(jnp.int32)
        first_row = jnp.sum(starts * is_mine).astype(jnp.int32)
        history = jnp.sum(history_len * is_mine).astype(jnp.int32)
        is_live = positions < new_count
        event_index = jnp.clip(first_row + positions, 0, ROWS - 1).astype(jnp.int32)
        event_rows = jnp.where(is_live[:, None, None], events[event_index], jnp.zeros((), events.dtype))
        queries = event_rows[:, 0].astype(jnp.float32).reshape(CAP, H, DH)
        own_keys = event_rows[:, 1].astype(jnp.float32).reshape(CAP, H, DH)
        own_values = event_rows[:, 2].astype(jnp.float32).reshape(CAP, H, DH)
        cache_rows = cache_kv[slot_index]
        key_rows = cache_rows[:, 0].astype(jnp.float32).reshape(HIST, H, DH)
        value_rows = cache_rows[:, 1].astype(jnp.float32).reshape(HIST, H, DH)
        scores = jnp.einsum('ehd,jhd->hej', queries, key_rows) * score_scale
        visible = jnp.arange(HIST, dtype=jnp.int32) < history
        weights = jnp.where(visible[None, None, :], jax.nn.silu(scores), 0.0).astype(jnp.bfloat16)
        weights = lax.optimization_barrier(weights).astype(jnp.float32)
        summed = jnp.einsum('hej,jhd->ehd', weights, value_rows)
        own_score = lax.optimization_barrier(jnp.sum(queries * own_keys, axis=-1)) * score_scale
        attended = (summed + jax.nn.silu(own_score)[:, :, None] * own_values) / (history + 1).astype(jnp.float32)
        attended = attended.reshape(CAP, HD)
        row_mean = lax.optimization_barrier(jnp.sum(attended, axis=-1)) / HD
        row_var = lax.optimization_barrier(jnp.sum(attended * attended, axis=-1)) / HD - row_mean * row_mean
        normed = (attended - row_mean[:, None]) * lax.rsqrt(row_var + EPSILON)[:, None]
        gated = (normed * event_rows[:, 3].astype(jnp.float32)).astype(jnp.bfloat16)
        mixed_rows = jnp.dot(gated, w_out, preferred_element_type=jnp.float32)
        layer_rows = jnp.where(is_live[:, None], mixed_rows, 0.0).astype(jnp.bfloat16)
        return (event_rows[:, 1:3], layer_rows)
    new_kv, layer_out = lax.map(per_owner, jnp.arange(USERS, dtype=jnp.int32))
    return (new_kv, layer_out)
```

```python
import functools
import math

import jax
import jax.numpy as jnp
from jax import lax
from jax.experimental import pallas as pl
from jax.experimental.pallas import tpu as pltpu
from jax.sharding import PartitionSpec as P

DH = 128
CAP = 640
TILE = 16


EPSILON = 1e-06


def normalize(attended, gate_rows, width_all):
    total_sum, total_squares = lax.psum(
        (jnp.sum(attended, axis=-1), jnp.sum(attended * attended, axis=-1)), "mp"
    )
    row_mean = total_sum / width_all
    row_var = total_squares / width_all - row_mean * row_mean
    normed = (attended - row_mean[:, None]) * lax.rsqrt(row_var + EPSILON)[:, None]
    return (normed * gate_rows.astype(jnp.float32)).astype(jnp.bfloat16)


def project(gated, w_out):
    return jnp.dot(
        lax.all_gather(gated, "mp", axis=1, tiled=True), w_out, preferred_element_type=jnp.float32
    )


def general_device(new_rows, counts, history_len, user_owner, cache_kv, w_out):
    dp_count = lax.axis_size("dp")
    my_index = lax.axis_index("dp")
    local_rows = new_rows.shape[0]
    per_peer = CAP // dp_count
    width_all = w_out.shape[0]
    user_ids = jnp.arange(counts.shape[0], dtype=jnp.int32)
    starts = jnp.cumsum(counts) - counts
    event_ids = jnp.arange(local_rows, dtype=jnp.int32) * dp_count + my_index
    row_user = jnp.sum((starts[None, :] <= event_ids[:, None]).astype(jnp.int32), axis=1) - 1
    one_hot = (user_ids[None, :] == row_user[:, None]).astype(jnp.int32)
    row_first = jnp.sum(one_hot * starts[None, :], axis=1)
    row_owner = jnp.sum(one_hot * user_owner[None, :], axis=1)
    position = (event_ids - row_first) // dp_count * dp_count + row_owner
    is_mine = (user_owner == my_index).astype(jnp.int32)
    new_count = jnp.sum(counts * is_mine)
    first_row = jnp.sum(starts * is_mine)
    history = jnp.sum(history_len * is_mine)
    is_live = jnp.arange(CAP, dtype=jnp.int32) < new_count
    event_rows = new_rows[:, 0]
    feature_here = event_rows.shape[-1]
    heads_here = feature_here // DH
    history_cap = cache_kv.shape[1]
    cache_keys = cache_kv[0, :, 0].reshape(history_cap, heads_here, DH)
    cache_values = cache_kv[0, :, 1].reshape(history_cap, heads_here, DH)
    score_scale = 1.0 / math.sqrt(DH)
    buffer = jnp.zeros((CAP,) + event_rows.shape[1:], event_rows.dtype).at[position].set(event_rows)
    arrived = lax.all_to_all(
        buffer.reshape((per_peer, dp_count) + event_rows.shape[1:]),
        "dp",
        split_axis=1,
        concat_axis=1,
        tiled=True,
    )
    ordered = jnp.roll(arrived, -first_row, axis=1).reshape((CAP,) + arrived.shape[2:])
    queries = ordered[:, 0].reshape(CAP, heads_here, DH)
    own_keys = ordered[:, 1].reshape(CAP, heads_here, DH)
    own_values = ordered[:, 2].reshape(CAP, heads_here, DH)
    scores = (
        jnp.einsum("ehd,jhd->hej", queries, cache_keys, preferred_element_type=jnp.float32)
        * score_scale
    )
    visible = jnp.arange(history_cap, dtype=jnp.int32) < history
    weights = jnp.where(visible[None, None, :], jax.nn.silu(scores), 0.0).astype(jnp.bfloat16)
    summed = jnp.einsum("hej,jhd->ehd", weights, cache_values, preferred_element_type=jnp.float32)
    own_score = (
        jnp.sum(queries.astype(jnp.float32) * own_keys.astype(jnp.float32), axis=-1) * score_scale
    )
    attended = (summed + jax.nn.silu(own_score)[:, :, None] * own_values.astype(jnp.float32)) / (
        history + 1
    ).astype(jnp.float32)
    attended = attended.reshape(CAP, feature_here)
    gated = normalize(attended, ordered[:, 3], width_all)
    mixed_rows = project(gated, w_out)
    results = jnp.where(is_live[:, None], mixed_rows, 0.0).astype(jnp.bfloat16)
    key_value = ordered[:, 1:3]
    return (key_value[None], results[None])


def half_silu(half):
    return half + half * jnp.tanh(half)


def layer_kernel(
    dp_count,
    mp_count,
    counts_ref,
    history_ref,
    owner_ref,
    rows_ref,
    cache_ref,
    w_ref,
    kv_ref,
    out_ref,
    send_buf,
    recv_buf,
    values_buf,
    perm_buf,
    attended_buf,
    gate_buf,
    stats_buf,
    gated_buf,
    row_send,
    row_recv,
    stats_send,
    stats_recv,
    gated_send,
    gated_recv,
):
    me = lax.axis_index("dp")
    my_part = lax.axis_index("mp")
    users = counts_ref.shape[0]
    local_rows = rows_ref.shape[0]
    width = w_ref.shape[1]
    width_all = w_ref.shape[0]
    heads = width // DH
    history_cap = cache_ref.shape[0]
    chunks = send_buf.shape[0]
    chunk = dp_count * TILE
    half_scale = 0.5 / math.sqrt(DH)

    def peer(step):
        return lax.rem(me + step, dp_count)

    def part(step):
        return lax.rem(my_part + step, mp_count)

    def row_copy(c, source, target):
        return pltpu.make_async_remote_copy(
            src_ref=send_buf.at[c, target],
            dst_ref=recv_buf.at[c, source],
            send_sem=row_send.at[c, target],
            recv_sem=row_recv.at[c, source],
            device_id=(target, my_part),
            device_id_type=pl.DeviceIdType.MESH,
        )

    def part_copy(buf, send_sem, recv_sem, c, source, target):
        return pltpu.make_async_remote_copy(
            src_ref=buf.at[c, source],
            dst_ref=buf.at[c, source],
            send_sem=send_sem.at[c, target],
            recv_sem=recv_sem.at[c, source],
            device_id=(me, target),
            device_id_type=pl.DeviceIdType.MESH,
        )

    barrier = pltpu.get_barrier_semaphore()
    for step in range(1, dp_count):
        pl.semaphore_signal(
            barrier, inc=1, device_id=(peer(step), my_part), device_id_type=pl.DeviceIdType.MESH
        )
    for step in range(1, mp_count):
        pl.semaphore_signal(
            barrier, inc=1, device_id=(me, part(step)), device_id_type=pl.DeviceIdType.MESH
        )

    slot_first = [jnp.int32(0)] * dp_count
    my_count = jnp.int32(0)
    my_first = jnp.int32(0)
    my_history = jnp.int32(0)
    first = jnp.int32(0)
    for user in range(users):
        count = counts_ref[user]
        owner = owner_ref[user]
        slot_first = [
            jnp.where(owner == slot, first, slot_first[slot]) for slot in range(dp_count)
        ]
        mine = owner == me
        my_count = jnp.where(mine, count, my_count)
        my_first = jnp.where(mine, first, my_first)
        my_history = jnp.where(mine, history_ref[user], my_history)
        first = first + count
    slot_row = [lax.div(value - me + (dp_count - 1), dp_count) for value in slot_first]

    row_id = lax.broadcasted_iota(jnp.int32, (TILE, local_rows), 1)
    tile_id = lax.broadcasted_iota(jnp.int32, (TILE, local_rows), 0)
    offset = row_id - tile_id

    pl.semaphore_wait(barrier, dp_count - 1 + mp_count - 1)

    def pack(c, carry):
        picked = jnp.concatenate(
            [
                jnp.where(offset == slot_row[slot] + c * TILE, 1.0, 0.0).astype(jnp.bfloat16)
                for slot in range(dp_count)
            ],
            axis=0,
        )
        sent = jnp.dot(picked, rows_ref[...], preferred_element_type=jnp.float32)
        send_buf[c] = sent.astype(jnp.bfloat16).reshape(dp_count, TILE, 4 * width)
        for step in range(1, dp_count):
            row_copy(c, me, peer(step)).start()
        recv_buf[c, me] = send_buf[c, me]
        return carry

    lax.fori_loop(0, chunks, pack, 0)

    place = lax.broadcasted_iota(jnp.int32, (chunk, chunk), 0)
    landed = lax.broadcasted_iota(jnp.int32, (chunk, chunk), 1)
    source_of = landed // TILE
    ordered_at = dp_count * (landed - source_of * TILE) + lax.rem(
        source_of - lax.rem(my_first, dp_count) + dp_count, dp_count
    )
    perm_buf[...] = jnp.where(place == ordered_at, 1.0, 0.0).astype(jnp.bfloat16)
    history_id = lax.broadcasted_iota(jnp.int32, (history_cap, width), 0)
    values_buf[...] = jnp.where(
        history_id < my_history, cache_ref[:, width:].astype(jnp.float32), 0.0
    ).astype(jnp.bfloat16)
    lane = lax.broadcasted_iota(jnp.int32, (chunk, 128), 1)
    chunk_row = lax.broadcasted_iota(jnp.int32, (chunk, 1), 0)
    inverse = 1.0 / (my_history + 1).astype(jnp.float32)

    def attend(c):
        for step in range(1, dp_count):
            row_copy(c, peer(step), me).wait_recv()
        arrived = recv_buf[c].reshape(chunk, 4 * width)
        ordered = jnp.dot(perm_buf[...], arrived, preferred_element_type=jnp.float32)
        here = pl.ds(pl.multiple_of(c * chunk, chunk), chunk)
        live = c * chunk + chunk_row < my_count
        kv_ref[here, :] = jnp.where(live, ordered[:, width : 3 * width], 0.0).astype(jnp.bfloat16)
        gate_buf[...] = ordered[:, 3 * width :]
        total = jnp.zeros((chunk, 1), jnp.float32)
        squares = jnp.zeros((chunk, 1), jnp.float32)
        for head in range(heads):
            columns = slice(head * DH, (head + 1) * DH)
            query = ordered[:, columns]
            key = ordered[:, width + head * DH : width + (head + 1) * DH]
            value = ordered[:, 2 * width + head * DH : 2 * width + (head + 1) * DH]
            half = (
                lax.dot_general(
                    query.astype(jnp.bfloat16),
                    cache_ref[:, columns],
                    (((1,), (1,)), ((), ())),
                    preferred_element_type=jnp.float32,
                )
                * half_scale
            )
            summed = jnp.dot(
                half_silu(half).astype(jnp.bfloat16),
                values_buf[:, columns],
                preferred_element_type=jnp.float32,
            )
            own = jnp.sum(query * key, axis=1, keepdims=True) * half_scale
            attended = (summed + half_silu(own) * value) * inverse
            attended_buf[:, columns] = attended
            total = total + jnp.sum(attended, axis=1, keepdims=True)
            squares = squares + jnp.sum(attended * attended, axis=1, keepdims=True)
        both = jnp.where(lane == 0, total, jnp.where(lane == 1, squares, 0.0))
        stats_buf[c, my_part] = both.T[:8]
        for step in range(1, mp_count):
            part_copy(stats_buf, stats_send, stats_recv, c, my_part, part(step)).start()

    def gate(c):
        for step in range(1, mp_count):
            part_copy(stats_buf, stats_send, stats_recv, c, part(step), my_part).wait_recv()
        stats = stats_buf[c, 0]
        for index in range(1, mp_count):
            stats = stats + stats_buf[c, index]
        stats = jnp.concatenate([stats, jnp.zeros((128 - 8, chunk), jnp.float32)], axis=0).T
        mean = stats[:, 0:1] / width_all
        variance = stats[:, 1:2] / width_all - mean * mean
        normed = (attended_buf[...] - mean) * lax.rsqrt(variance + EPSILON)
        gated_buf[c, my_part] = (normed * gate_buf[...]).astype(jnp.bfloat16)
        for step in range(1, mp_count):
            part_copy(gated_buf, gated_send, gated_recv, c, my_part, part(step)).start()

    def mix(c):
        for step in range(1, mp_count):
            part_copy(gated_buf, gated_send, gated_recv, c, part(step), my_part).wait_recv()
        mixed = jnp.zeros((chunk, width), jnp.float32)
        for index in range(mp_count):
            mixed = mixed + jnp.dot(
                gated_buf[c, index],
                w_ref[index * width : (index + 1) * width, :],
                preferred_element_type=jnp.float32,
            )
        here = pl.ds(pl.multiple_of(c * chunk, chunk), chunk)
        live = c * chunk + chunk_row < my_count
        out_ref[here, :] = jnp.where(live, mixed, 0.0).astype(jnp.bfloat16)

    def work(c, carry):
        attend(c)

        @pl.when(c > 0)
        def _():
            mix(c - 1)

        gate(c)
        return carry

    lax.fori_loop(0, chunks, work, 0)
    mix(chunks - 1)

    def finish(c, carry):
        for step in range(1, dp_count):
            row_copy(c, me, peer(step)).wait_send()
        for step in range(1, mp_count):
            part_copy(stats_buf, stats_send, stats_recv, c, my_part, part(step)).wait_send()
            part_copy(gated_buf, gated_send, gated_recv, c, my_part, part(step)).wait_send()
        return carry

    lax.fori_loop(0, chunks, finish, 0)


def kernel_device(new_rows, counts, history_len, user_owner, cache_kv, w_out):
    dp_count = lax.axis_size("dp")
    mp_count = lax.axis_size("mp")
    width = w_out.shape[1]
    local_rows = new_rows.shape[0]
    history_cap = cache_kv.shape[1]
    chunks = CAP // (dp_count * TILE)
    chunk = dp_count * TILE
    smem = pl.BlockSpec(memory_space=pltpu.SMEM)
    vmem = pl.BlockSpec(memory_space=pltpu.VMEM)
    dma = pltpu.SemaphoreType.DMA
    key_value, results = pl.pallas_call(
        functools.partial(layer_kernel, dp_count, mp_count),
        out_shape=(
            jax.ShapeDtypeStruct((CAP, 2 * width), jnp.bfloat16),
            jax.ShapeDtypeStruct((CAP, width), jnp.bfloat16),
        ),
        in_specs=[smem, smem, smem, vmem, vmem, vmem],
        out_specs=(vmem, vmem),
        scratch_shapes=[
            pltpu.VMEM((chunks, dp_count, TILE, 4 * width), jnp.bfloat16),
            pltpu.VMEM((chunks, dp_count, TILE, 4 * width), jnp.bfloat16),
            pltpu.VMEM((history_cap, width), jnp.bfloat16),
            pltpu.VMEM((chunk, chunk), jnp.bfloat16),
            pltpu.VMEM((chunk, width), jnp.float32),
            pltpu.VMEM((chunk, width), jnp.float32),
            pltpu.VMEM((chunks, mp_count, 8, chunk), jnp.float32),
            pltpu.VMEM((chunks, mp_count, chunk, width), jnp.bfloat16),
            dma((chunks, dp_count)),
            dma((chunks, dp_count)),
            dma((chunks, mp_count)),
            dma((chunks, mp_count)),
            dma((chunks, mp_count)),
            dma((chunks, mp_count)),
        ],
        compiler_params=pltpu.CompilerParams(
            collective_id=0, has_side_effects=True, vmem_limit_bytes=40 * 2**20
        ),
    )(
        counts,
        history_len,
        user_owner,
        new_rows.reshape(local_rows, 4 * width),
        cache_kv.reshape(history_cap, 2 * width),
        w_out,
    )
    return (key_value.reshape(1, CAP, 2, width), results[None])


def solution(mesh):
    placed = (P(None, "dp", None, "mp"), P(), P(), P(), P("dp", None, None, "mp"), P(None, "mp"))
    fits = mesh.shape["dp"] * TILE == 128
    return jax.shard_map(
        kernel_device if fits else general_device,
        mesh=mesh,
        in_specs=placed,
        out_specs=(P("dp", None, None, "mp"), P("dp", None, "mp")),
        check_vma=False,
    )
```

```python
import functools
import math

import jax
import jax.numpy as jnp
from jax import lax
from jax.experimental import pallas as pl
from jax.experimental.pallas import tpu as pltpu
from jax.sharding import PartitionSpec as P

DH = 128
CAP = 640
TILE = 16
EVENTS = 8


EPSILON = 1e-06


def normalize(attended, gate_rows, width_all):
    total_sum, total_squares = lax.psum(
        (jnp.sum(attended, axis=-1), jnp.sum(attended * attended, axis=-1)), "mp"
    )
    row_mean = total_sum / width_all
    row_var = total_squares / width_all - row_mean * row_mean
    normed = (attended - row_mean[:, None]) * lax.rsqrt(row_var + EPSILON)[:, None]
    return (normed * gate_rows.astype(jnp.float32)).astype(jnp.bfloat16)


def project(gated, w_out):
    return jnp.dot(
        lax.all_gather(gated, "mp", axis=1, tiled=True), w_out, preferred_element_type=jnp.float32
    )


def general_device(new_rows, counts, history_len, user_owner, cache_kv, w_out):
    dp_count = lax.axis_size("dp")
    my_index = lax.axis_index("dp")
    local_rows = new_rows.shape[0]
    per_peer = CAP // dp_count
    width_all = w_out.shape[0]
    user_ids = jnp.arange(counts.shape[0], dtype=jnp.int32)
    starts = jnp.cumsum(counts) - counts
    event_ids = jnp.arange(local_rows, dtype=jnp.int32) * dp_count + my_index
    row_user = jnp.sum((starts[None, :] <= event_ids[:, None]).astype(jnp.int32), axis=1) - 1
    one_hot = (user_ids[None, :] == row_user[:, None]).astype(jnp.int32)
    row_first = jnp.sum(one_hot * starts[None, :], axis=1)
    row_owner = jnp.sum(one_hot * user_owner[None, :], axis=1)
    position = (event_ids - row_first) // dp_count * dp_count + row_owner
    is_mine = (user_owner == my_index).astype(jnp.int32)
    new_count = jnp.sum(counts * is_mine)
    first_row = jnp.sum(starts * is_mine)
    history = jnp.sum(history_len * is_mine)
    is_live = jnp.arange(CAP, dtype=jnp.int32) < new_count
    event_rows = new_rows[:, 0]
    feature_here = event_rows.shape[-1]
    heads_here = feature_here // DH
    history_cap = cache_kv.shape[1]
    cache_keys = cache_kv[0, :, 0].reshape(history_cap, heads_here, DH)
    cache_values = cache_kv[0, :, 1].reshape(history_cap, heads_here, DH)
    score_scale = 1.0 / math.sqrt(DH)
    buffer = jnp.zeros((CAP,) + event_rows.shape[1:], event_rows.dtype).at[position].set(event_rows)
    arrived = lax.all_to_all(
        buffer.reshape((per_peer, dp_count) + event_rows.shape[1:]),
        "dp",
        split_axis=1,
        concat_axis=1,
        tiled=True,
    )
    ordered = jnp.roll(arrived, -first_row, axis=1).reshape((CAP,) + arrived.shape[2:])
    queries = ordered[:, 0].reshape(CAP, heads_here, DH)
    own_keys = ordered[:, 1].reshape(CAP, heads_here, DH)
    own_values = ordered[:, 2].reshape(CAP, heads_here, DH)
    scores = (
        jnp.einsum("ehd,jhd->hej", queries, cache_keys, preferred_element_type=jnp.float32)
        * score_scale
    )
    visible = jnp.arange(history_cap, dtype=jnp.int32) < history
    weights = jnp.where(visible[None, None, :], jax.nn.silu(scores), 0.0).astype(jnp.bfloat16)
    summed = jnp.einsum("hej,jhd->ehd", weights, cache_values, preferred_element_type=jnp.float32)
    own_score = (
        jnp.sum(queries.astype(jnp.float32) * own_keys.astype(jnp.float32), axis=-1) * score_scale
    )
    attended = (summed + jax.nn.silu(own_score)[:, :, None] * own_values.astype(jnp.float32)) / (
        history + 1
    ).astype(jnp.float32)
    attended = attended.reshape(CAP, feature_here)
    gated = normalize(attended, ordered[:, 3], width_all)
    mixed_rows = project(gated, w_out)
    results = jnp.where(is_live[:, None], mixed_rows, 0.0).astype(jnp.bfloat16)
    key_value = ordered[:, 1:3]
    return (key_value[None], results[None])


def half_silu(half):
    return half + half * jnp.tanh(half)


def layer_kernel(
    dp_count,
    mp_count,
    counts_ref,
    history_ref,
    owner_ref,
    rows_ref,
    cache_ref,
    w_ref,
    kv_ref,
    out_ref,
    w_buf,
    send_buf,
    recv_buf,
    values_buf,
    perm_buf,
    attended_buf,
    gate_buf,
    stats_buf,
    gated_buf,
    row_send,
    row_recv,
    stats_send,
    stats_recv,
    gated_send,
    gated_recv,
    w_sem,
):
    fetch_w = pltpu.make_async_copy(w_ref, w_buf, w_sem)
    fetch_w.start()
    me = lax.axis_index("dp")
    my_part = lax.axis_index("mp")
    users = counts_ref.shape[0]
    local_rows = rows_ref.shape[0]
    width = w_ref.shape[1]
    width_all = w_ref.shape[0]
    heads = width // DH
    history_cap = cache_ref.shape[0]
    chunks = send_buf.shape[0]
    chunk = dp_count * EVENTS
    half_scale = 0.5 / math.sqrt(DH)

    def peer(step):
        return lax.rem(me + step, dp_count)

    def part(step):
        return lax.rem(my_part + step, mp_count)

    def row_copy(c, source, target):
        return pltpu.make_async_remote_copy(
            src_ref=send_buf.at[c, target],
            dst_ref=recv_buf.at[c, source],
            send_sem=row_send.at[c, target],
            recv_sem=row_recv.at[c, source],
            device_id=(target, my_part),
            device_id_type=pl.DeviceIdType.MESH,
        )

    def part_copy(buf, send_sem, recv_sem, c, source, target):
        return pltpu.make_async_remote_copy(
            src_ref=buf.at[c, source],
            dst_ref=buf.at[c, source],
            send_sem=send_sem.at[c, target],
            recv_sem=recv_sem.at[c, source],
            device_id=(me, target),
            device_id_type=pl.DeviceIdType.MESH,
        )

    barrier = pltpu.get_barrier_semaphore()
    for step in range(1, dp_count):
        pl.semaphore_signal(
            barrier, inc=1, device_id=(peer(step), my_part), device_id_type=pl.DeviceIdType.MESH
        )
    for step in range(1, mp_count):
        pl.semaphore_signal(
            barrier, inc=1, device_id=(me, part(step)), device_id_type=pl.DeviceIdType.MESH
        )

    slot_first = [jnp.int32(0)] * dp_count
    my_count = jnp.int32(0)
    my_first = jnp.int32(0)
    my_history = jnp.int32(0)
    first = jnp.int32(0)
    for user in range(users):
        count = counts_ref[user]
        owner = owner_ref[user]
        slot_first = [
            jnp.where(owner == slot, first, slot_first[slot]) for slot in range(dp_count)
        ]
        mine = owner == me
        my_count = jnp.where(mine, count, my_count)
        my_first = jnp.where(mine, first, my_first)
        my_history = jnp.where(mine, history_ref[user], my_history)
        first = first + count
    slot_row = [lax.div(value - me + (dp_count - 1), dp_count) for value in slot_first]

    row_id = lax.broadcasted_iota(jnp.int32, (TILE, local_rows), 1)
    tile_id = lax.broadcasted_iota(jnp.int32, (TILE, local_rows), 0)
    offset = row_id - lax.rem(tile_id, EVENTS)
    upper = lax.broadcasted_iota(jnp.int32, (dp_count, TILE, 2 * width), 1) < EVENTS

    def pack(c):
        picked = jnp.concatenate(
            [
                jnp.where(offset == slot_row[slot] + c * EVENTS, 1.0, 0.0).astype(jnp.bfloat16)
                for slot in range(dp_count)
            ],
            axis=0,
        )
        sent = jnp.dot(picked, rows_ref[...], preferred_element_type=jnp.float32)
        sent = sent.reshape(dp_count, TILE, 4 * width)
        send_buf[c] = jnp.where(upper, sent[:, :, : 2 * width], sent[:, :, 2 * width :]).astype(
            jnp.bfloat16
        )

    def post(c):
        for step in range(1, dp_count):
            row_copy(c, me, peer(step)).start()
        recv_buf[c, me] = send_buf[c, me]

    def pack_and_post(c, carry):
        pack(c)
        post(c)
        return carry

    pack(0)
    pl.semaphore_wait(barrier, dp_count - 1 + mp_count - 1)
    post(0)
    lax.fori_loop(1, chunks, pack_and_post, 0)

    place = lax.broadcasted_iota(jnp.int32, (2 * chunk, 2 * chunk), 0)
    landed = lax.broadcasted_iota(jnp.int32, (2 * chunk, 2 * chunk), 1)
    source_of = landed // TILE
    ordered_at = dp_count * (landed - source_of * TILE) + lax.rem(
        source_of - lax.rem(my_first, dp_count) + dp_count, dp_count
    )
    perm_buf[...] = jnp.where(place == ordered_at, 1.0, 0.0).astype(jnp.bfloat16)
    history_id = lax.broadcasted_iota(jnp.int32, (history_cap, width), 0)
    values_buf[...] = jnp.where(
        history_id < my_history, cache_ref[:, width:].astype(jnp.float32), 0.0
    ).astype(jnp.bfloat16)
    lane = lax.broadcasted_iota(jnp.int32, (chunk, 128), 1)
    chunk_row = lax.broadcasted_iota(jnp.int32, (chunk, 1), 0)
    inverse = 1.0 / (my_history + 1).astype(jnp.float32)

    def attend(c):
        for step in range(1, dp_count):
            row_copy(c, peer(step), me).wait_recv()
        arrived = recv_buf[c].reshape(2 * chunk, 2 * width)
        ordered = jnp.dot(perm_buf[...], arrived, preferred_element_type=jnp.float32)
        query_key, value_gate = ordered[:chunk], ordered[chunk:]
        here = pl.ds(pl.multiple_of(c * chunk, chunk), chunk)
        live = c * chunk + chunk_row < my_count
        kv_ref[here, :width] = jnp.where(live, query_key[:, width:], 0.0).astype(jnp.bfloat16)
        kv_ref[here, width:] = jnp.where(live, value_gate[:, :width], 0.0).astype(jnp.bfloat16)
        gate_buf[...] = value_gate[:, width:]
        total = jnp.zeros((chunk, 1), jnp.float32)
        squares = jnp.zeros((chunk, 1), jnp.float32)
        for head in range(heads):
            columns = slice(head * DH, (head + 1) * DH)
            query = query_key[:, columns]
            key = query_key[:, width + head * DH : width + (head + 1) * DH]
            value = value_gate[:, columns]
            half = (
                lax.dot_general(
                    query.astype(jnp.bfloat16),
                    cache_ref[:, columns],
                    (((1,), (1,)), ((), ())),
                    preferred_element_type=jnp.float32,
                )
                * half_scale
            )
            summed = jnp.dot(
                half_silu(half).astype(jnp.bfloat16),
                values_buf[:, columns],
                preferred_element_type=jnp.float32,
            )
            own = jnp.sum(query * key, axis=1, keepdims=True) * half_scale
            attended = (summed + half_silu(own) * value) * inverse
            attended_buf[:, columns] = attended
            total = total + jnp.sum(attended, axis=1, keepdims=True)
            squares = squares + jnp.sum(attended * attended, axis=1, keepdims=True)
        both = jnp.where(lane == 0, total, jnp.where(lane == 1, squares, 0.0))
        both = jnp.concatenate([both, jnp.zeros((128 - chunk, 128), jnp.float32)], axis=0)
        stats_buf[c, my_part] = both.T[:8]
        for step in range(1, mp_count):
            part_copy(stats_buf, stats_send, stats_recv, c, my_part, part(step)).start()

    def gate(c):
        for step in range(1, mp_count):
            part_copy(stats_buf, stats_send, stats_recv, c, part(step), my_part).wait_recv()
        stats = stats_buf[c, 0]
        for index in range(1, mp_count):
            stats = stats + stats_buf[c, index]
        stats = jnp.concatenate([stats, jnp.zeros((128 - 8, 128), jnp.float32)], axis=0).T
        mean = stats[:chunk, 0:1] / width_all
        variance = stats[:chunk, 1:2] / width_all - mean * mean
        normed = (attended_buf[...] - mean) * lax.rsqrt(variance + EPSILON)
        gated_buf[c, my_part] = (normed * gate_buf[...]).astype(jnp.bfloat16)
        for step in range(1, mp_count):
            part_copy(gated_buf, gated_send, gated_recv, c, my_part, part(step)).start()

    def mix(c):
        for step in range(1, mp_count):
            part_copy(gated_buf, gated_send, gated_recv, c, part(step), my_part).wait_recv()
        mixed = jnp.zeros((chunk, width), jnp.float32)
        for index in range(mp_count):
            mixed = mixed + jnp.dot(
                gated_buf[c, index],
                w_buf[index * width : (index + 1) * width, :],
                preferred_element_type=jnp.float32,
            )
        here = pl.ds(pl.multiple_of(c * chunk, chunk), chunk)
        live = c * chunk + chunk_row < my_count
        out_ref[here, :] = jnp.where(live, mixed, 0.0).astype(jnp.bfloat16)

    def work(c, carry):
        attend(c)

        @pl.when(c == 1)
        def _():
            fetch_w.wait()

        @pl.when(c > 0)
        def _():
            mix(c - 1)

        gate(c)
        return carry

    lax.fori_loop(0, chunks, work, 0)
    mix(chunks - 1)

    def finish(c, carry):
        for step in range(1, dp_count):
            row_copy(c, me, peer(step)).wait_send()
        for step in range(1, mp_count):
            part_copy(stats_buf, stats_send, stats_recv, c, my_part, part(step)).wait_send()
            part_copy(gated_buf, gated_send, gated_recv, c, my_part, part(step)).wait_send()
        return carry

    lax.fori_loop(0, chunks, finish, 0)


def kernel_device(new_rows, counts, history_len, user_owner, cache_kv, w_out):
    dp_count = lax.axis_size("dp")
    mp_count = lax.axis_size("mp")
    width = w_out.shape[1]
    local_rows = new_rows.shape[0]
    history_cap = cache_kv.shape[1]
    chunks = CAP // (dp_count * EVENTS)
    chunk = dp_count * EVENTS
    smem = pl.BlockSpec(memory_space=pltpu.SMEM)
    vmem = pl.BlockSpec(memory_space=pltpu.VMEM)
    dma = pltpu.SemaphoreType.DMA
    key_value, results = pl.pallas_call(
        functools.partial(layer_kernel, dp_count, mp_count),
        out_shape=(
            jax.ShapeDtypeStruct((CAP, 2 * width), jnp.bfloat16),
            jax.ShapeDtypeStruct((CAP, width), jnp.bfloat16),
        ),
        in_specs=[smem, smem, smem, vmem, vmem, pl.BlockSpec(memory_space=pltpu.HBM)],
        out_specs=(vmem, vmem),
        scratch_shapes=[
            pltpu.VMEM(w_out.shape, jnp.bfloat16),
            pltpu.VMEM((chunks, dp_count, TILE, 2 * width), jnp.bfloat16),
            pltpu.VMEM((chunks, dp_count, TILE, 2 * width), jnp.bfloat16),
            pltpu.VMEM((history_cap, width), jnp.bfloat16),
            pltpu.VMEM((2 * chunk, 2 * chunk), jnp.bfloat16),
            pltpu.VMEM((chunk, width), jnp.float32),
            pltpu.VMEM((chunk, width), jnp.float32),
            pltpu.VMEM((chunks, mp_count, 8, 128), jnp.float32),
            pltpu.VMEM((chunks, mp_count, chunk, width), jnp.bfloat16),
            dma((chunks, dp_count)),
            dma((chunks, dp_count)),
            dma((chunks, mp_count)),
            dma((chunks, mp_count)),
            dma((chunks, mp_count)),
            dma((chunks, mp_count)),
            dma,
        ],
        compiler_params=pltpu.CompilerParams(
            collective_id=0, has_side_effects=True, vmem_limit_bytes=40 * 2**20
        ),
    )(
        counts,
        history_len,
        user_owner,
        new_rows.reshape(local_rows, 4 * width),
        cache_kv.reshape(history_cap, 2 * width),
        w_out,
    )
    return (key_value.reshape(1, CAP, 2, width), results[None])


def solution(mesh):
    placed = (P(None, "dp", None, "mp"), P(), P(), P(), P("dp", None, None, "mp"), P(None, "mp"))
    fits = mesh.shape["dp"] * TILE == 128
    return jax.shard_map(
        kernel_device if fits else general_device,
        mesh=mesh,
        in_specs=placed,
        out_specs=(P("dp", None, None, "mp"), P("dp", None, "mp")),
        check_vma=False,
    )
```

```python
import functools
import itertools
import math

import jax
import jax.numpy as jnp
from jax import lax
from jax.experimental import pallas as pl
from jax.experimental.pallas import tpu as pltpu
from jax.sharding import PartitionSpec as P

DH = 128
CAP = 640
TILE = 16


EPSILON = 1e-06


def normalize(attended, gate_rows, width_all):
    total_sum, total_squares = lax.psum(
        (jnp.sum(attended, axis=-1), jnp.sum(attended * attended, axis=-1)), "mp"
    )
    row_mean = total_sum / width_all
    row_var = total_squares / width_all - row_mean * row_mean
    normed = (attended - row_mean[:, None]) * lax.rsqrt(row_var + EPSILON)[:, None]
    return (normed * gate_rows.astype(jnp.float32)).astype(jnp.bfloat16)


def project(gated, w_out):
    return jnp.dot(
        lax.all_gather(gated, "mp", axis=1, tiled=True), w_out, preferred_element_type=jnp.float32
    )


def general_device(new_rows, counts, history_len, user_owner, cache_kv, w_out):
    dp_count = lax.axis_size("dp")
    my_index = lax.axis_index("dp")
    local_rows = new_rows.shape[0]
    per_peer = CAP // dp_count
    width_all = w_out.shape[0]
    user_ids = jnp.arange(counts.shape[0], dtype=jnp.int32)
    starts = jnp.cumsum(counts) - counts
    event_ids = jnp.arange(local_rows, dtype=jnp.int32) * dp_count + my_index
    row_user = jnp.sum((starts[None, :] <= event_ids[:, None]).astype(jnp.int32), axis=1) - 1
    one_hot = (user_ids[None, :] == row_user[:, None]).astype(jnp.int32)
    row_first = jnp.sum(one_hot * starts[None, :], axis=1)
    row_owner = jnp.sum(one_hot * user_owner[None, :], axis=1)
    position = (event_ids - row_first) // dp_count * dp_count + row_owner
    is_mine = (user_owner == my_index).astype(jnp.int32)
    new_count = jnp.sum(counts * is_mine)
    first_row = jnp.sum(starts * is_mine)
    history = jnp.sum(history_len * is_mine)
    is_live = jnp.arange(CAP, dtype=jnp.int32) < new_count
    event_rows = new_rows[:, 0]
    feature_here = event_rows.shape[-1]
    heads_here = feature_here // DH
    history_cap = cache_kv.shape[1]
    cache_keys = cache_kv[0, :, 0].reshape(history_cap, heads_here, DH)
    cache_values = cache_kv[0, :, 1].reshape(history_cap, heads_here, DH)
    score_scale = 1.0 / math.sqrt(DH)
    buffer = jnp.zeros((CAP,) + event_rows.shape[1:], event_rows.dtype).at[position].set(event_rows)
    arrived = lax.all_to_all(
        buffer.reshape((per_peer, dp_count) + event_rows.shape[1:]),
        "dp",
        split_axis=1,
        concat_axis=1,
        tiled=True,
    )
    ordered = jnp.roll(arrived, -first_row, axis=1).reshape((CAP,) + arrived.shape[2:])
    queries = ordered[:, 0].reshape(CAP, heads_here, DH)
    own_keys = ordered[:, 1].reshape(CAP, heads_here, DH)
    own_values = ordered[:, 2].reshape(CAP, heads_here, DH)
    scores = (
        jnp.einsum("ehd,jhd->hej", queries, cache_keys, preferred_element_type=jnp.float32)
        * score_scale
    )
    visible = jnp.arange(history_cap, dtype=jnp.int32) < history
    weights = jnp.where(visible[None, None, :], jax.nn.silu(scores), 0.0).astype(jnp.bfloat16)
    summed = jnp.einsum("hej,jhd->ehd", weights, cache_values, preferred_element_type=jnp.float32)
    own_score = (
        jnp.sum(queries.astype(jnp.float32) * own_keys.astype(jnp.float32), axis=-1) * score_scale
    )
    attended = (summed + jax.nn.silu(own_score)[:, :, None] * own_values.astype(jnp.float32)) / (
        history + 1
    ).astype(jnp.float32)
    attended = attended.reshape(CAP, feature_here)
    gated = normalize(attended, ordered[:, 3], width_all)
    mixed_rows = project(gated, w_out)
    results = jnp.where(is_live[:, None], mixed_rows, 0.0).astype(jnp.bfloat16)
    key_value = ordered[:, 1:3]
    return (key_value[None], results[None])


def half_silu(half):
    return half + half * jnp.tanh(half)


def layer_kernel(
    dp_count,
    mp_count,
    base,
    large,
    counts_ref,
    history_ref,
    owner_ref,
    rows_ref,
    cache_ref,
    w_ref,
    kv_ref,
    out_ref,
    w_buf,
    send_buf,
    recv_buf,
    keys_buf,
    values_buf,
    perm_buf,
    attended_buf,
    gate_buf,
    stats_buf,
    gated_buf,
    row_send,
    row_recv,
    stats_send,
    stats_recv,
    gated_send,
    gated_recv,
    w_sem,
):
    fetch_w = pltpu.make_async_copy(w_ref, w_buf, w_sem)
    fetch_w.start()
    me = lax.axis_index("dp")
    my_part = lax.axis_index("mp")
    users = counts_ref.shape[0]
    local_rows = rows_ref.shape[0]
    width = w_ref.shape[1]
    width_all = w_ref.shape[0]
    heads = width // DH
    history_cap = cache_ref.shape[0]
    chunks = send_buf.shape[0]
    chunk = dp_count * TILE
    half_scale = 0.5 / math.sqrt(DH)
    is_large = functools.reduce(jnp.logical_or, [me == slot for slot in large])

    def peer(step):
        return lax.rem(me + step, dp_count)

    def part(step):
        return lax.rem(my_part + step, mp_count)

    def row_copy(c, source, target):
        return pltpu.make_async_remote_copy(
            src_ref=send_buf.at[c, target],
            dst_ref=recv_buf.at[c, source],
            send_sem=row_send.at[c, target],
            recv_sem=row_recv.at[c, source],
            device_id=(target, my_part),
            device_id_type=pl.DeviceIdType.MESH,
        )

    def part_copy(buf, send_sem, recv_sem, c, source, target):
        return pltpu.make_async_remote_copy(
            src_ref=buf.at[c, source],
            dst_ref=buf.at[c, source],
            send_sem=send_sem.at[c, target],
            recv_sem=recv_sem.at[c, source],
            device_id=(me, target),
            device_id_type=pl.DeviceIdType.MESH,
        )

    barrier = pltpu.get_barrier_semaphore()
    for step in range(1, dp_count):
        pl.semaphore_signal(
            barrier, inc=1, device_id=(peer(step), my_part), device_id_type=pl.DeviceIdType.MESH
        )
    for step in range(1, mp_count):
        pl.semaphore_signal(
            barrier, inc=1, device_id=(me, part(step)), device_id_type=pl.DeviceIdType.MESH
        )

    slot_first = [jnp.int32(0)] * dp_count
    my_count = jnp.int32(0)
    my_first = jnp.int32(0)
    my_history = jnp.int32(0)
    first = jnp.int32(0)
    for user in range(users):
        count = counts_ref[user]
        owner = owner_ref[user]
        slot_first = [
            jnp.where(owner == slot, first, slot_first[slot]) for slot in range(dp_count)
        ]
        mine = owner == me
        my_count = jnp.where(mine, count, my_count)
        my_first = jnp.where(mine, first, my_first)
        my_history = jnp.where(mine, history_ref[user], my_history)
        first = first + count
    slot_row = [lax.div(value - me + (dp_count - 1), dp_count) for value in slot_first]

    row_id = lax.broadcasted_iota(jnp.int32, (TILE, local_rows), 1)
    tile_id = lax.broadcasted_iota(jnp.int32, (TILE, local_rows), 0)
    offset = row_id - tile_id

    def pack(c, slots):
        picked = jnp.concatenate(
            [
                jnp.where(offset == slot_row[slot] + c * TILE, 1.0, 0.0).astype(jnp.bfloat16)
                for slot in slots
            ],
            axis=0,
        )
        sent = jnp.dot(picked, rows_ref[...], preferred_element_type=jnp.float32)
        return sent.astype(jnp.bfloat16).reshape(len(slots), TILE, 4 * width)

    def post(c):
        for step in range(1, dp_count):
            row_copy(c, me, peer(step)).start()
        recv_buf[c, me] = send_buf[c, me]

    def pack_all(c, carry):
        send_buf[c] = pack(c, range(dp_count))
        post(c)
        return carry

    def pack_large(c, carry):
        sent = pack(c, large)
        for index, slot in enumerate(large):
            send_buf[c, slot] = sent[index]

            @pl.when(me != slot)
            def _():
                row_copy(c, me, slot).start()

            @pl.when(me == slot)
            def _():
                recv_buf[c, slot] = send_buf[c, slot]

        return carry

    send_buf[0] = pack(0, range(dp_count))
    pl.semaphore_wait(barrier, dp_count - 1 + mp_count - 1)
    post(0)
    lax.fori_loop(1, base, pack_all, 0)
    if base < chunks:
        lax.fori_loop(base, chunks, pack_large, 0)

    place = lax.broadcasted_iota(jnp.int32, (chunk, chunk), 0)
    landed = lax.broadcasted_iota(jnp.int32, (chunk, chunk), 1)
    source_of = landed // TILE
    ordered_at = dp_count * (landed - source_of * TILE) + lax.rem(
        source_of - lax.rem(my_first, dp_count) + dp_count, dp_count
    )
    perm_buf[...] = jnp.where(place == ordered_at, 1.0, 0.0).astype(jnp.bfloat16)
    keys_buf[...] = cache_ref[:, :width].astype(jnp.float32).T.astype(jnp.bfloat16)
    history_id = lax.broadcasted_iota(jnp.int32, (history_cap, width), 0)
    values_buf[...] = jnp.where(
        history_id < my_history, cache_ref[:, width:].astype(jnp.float32), 0.0
    ).astype(jnp.bfloat16)
    line = lax.broadcasted_iota(jnp.int32, (8, chunk), 0)
    chunk_row = lax.broadcasted_iota(jnp.int32, (chunk, 1), 0)
    inverse = 1.0 / (my_history + 1).astype(jnp.float32)

    def attend(c):
        for step in range(1, dp_count):
            row_copy(c, peer(step), me).wait_recv()
        arrived = recv_buf[c].reshape(chunk, 4 * width)
        ordered = jnp.dot(perm_buf[...], arrived, preferred_element_type=jnp.float32)
        here = pl.ds(pl.multiple_of(c * chunk, chunk), chunk)
        live = c * chunk + chunk_row < my_count
        kv_ref[here, :] = jnp.where(live, ordered[:, width : 3 * width], 0.0).astype(jnp.bfloat16)
        gate_buf[...] = ordered[:, 3 * width :]
        total = jnp.zeros((chunk, DH), jnp.float32)
        squares = jnp.zeros((chunk, DH), jnp.float32)
        for head in range(heads):
            columns = slice(head * DH, (head + 1) * DH)
            query = ordered[:, columns]
            key = ordered[:, width + head * DH : width + (head + 1) * DH]
            value = ordered[:, 2 * width + head * DH : 2 * width + (head + 1) * DH]
            half = (
                jnp.dot(
                    query.astype(jnp.bfloat16),
                    keys_buf[columns, :],
                    preferred_element_type=jnp.float32,
                )
                * half_scale
            )
            summed = jnp.dot(
                half_silu(half).astype(jnp.bfloat16),
                values_buf[:, columns],
                preferred_element_type=jnp.float32,
            )
            own = jnp.sum(query * key, axis=1, keepdims=True) * half_scale
            attended = (summed + half_silu(own) * value) * inverse
            attended_buf[:, columns] = attended
            total = total + attended
            squares = squares + attended * attended
        total = jnp.sum(total.T, axis=0, keepdims=True)
        squares = jnp.sum(squares.T, axis=0, keepdims=True)
        stats_buf[c, my_part] = jnp.where(line == 0, total, jnp.where(line == 1, squares, 0.0))
        for step in range(1, mp_count):
            part_copy(stats_buf, stats_send, stats_recv, c, my_part, part(step)).start()

    def gate(c):
        for step in range(1, mp_count):
            part_copy(stats_buf, stats_send, stats_recv, c, part(step), my_part).wait_recv()
        stats = stats_buf[c, 0]
        for index in range(1, mp_count):
            stats = stats + stats_buf[c, index]
        mean = stats[0:1] / width_all
        variance = stats[1:2] / width_all - mean * mean
        stats = jnp.where(line == 0, mean, lax.rsqrt(variance + EPSILON))
        stats = jnp.concatenate([stats, jnp.zeros((128 - 8, chunk), jnp.float32)], axis=0).T
        normed = (attended_buf[...] - stats[:, 0:1]) * stats[:, 1:2]
        gated_buf[c, my_part] = (normed * gate_buf[...]).astype(jnp.bfloat16)
        for step in range(1, mp_count):
            part_copy(gated_buf, gated_send, gated_recv, c, my_part, part(step)).start()

    def mix(c):
        for step in range(1, mp_count):
            part_copy(gated_buf, gated_send, gated_recv, c, part(step), my_part).wait_recv()
        mixed = jnp.zeros((chunk, width), jnp.float32)
        for index in range(mp_count):
            mixed = mixed + jnp.dot(
                gated_buf[c, index],
                w_buf[index * width : (index + 1) * width, :],
                preferred_element_type=jnp.float32,
            )
        here = pl.ds(pl.multiple_of(c * chunk, chunk), chunk)
        live = c * chunk + chunk_row < my_count
        out_ref[here, :] = jnp.where(live, mixed, 0.0).astype(jnp.bfloat16)

    def work(c, carry):
        attend(c)

        @pl.when(c > 0)
        def _():
            mix(c - 1)

        gate(c)
        return carry

    lax.fori_loop(0, 1, work, 0)
    fetch_w.wait()
    lax.fori_loop(1, base, work, 0)
    if base < chunks:

        @pl.when(is_large)
        def _():
            lax.fori_loop(base, chunks, work, 0)
            mix(chunks - 1)

        @pl.when(jnp.logical_not(is_large))
        def _():
            mix(base - 1)
            kv_ref[base * chunk :, :] = jnp.zeros(
                ((chunks - base) * chunk, 2 * width), jnp.bfloat16
            )
            out_ref[base * chunk :, :] = jnp.zeros(((chunks - base) * chunk, width), jnp.bfloat16)

    else:
        mix(chunks - 1)

    def finish_parts(c, carry):
        for step in range(1, mp_count):
            part_copy(stats_buf, stats_send, stats_recv, c, my_part, part(step)).wait_send()
            part_copy(gated_buf, gated_send, gated_recv, c, my_part, part(step)).wait_send()
        return carry

    def finish_rows(c, carry):
        for step in range(1, dp_count):
            row_copy(c, me, peer(step)).wait_send()
        return carry

    def finish_large(c, carry):
        for slot in large:

            @pl.when(me != slot)
            def _():
                row_copy(c, me, slot).wait_send()

        return carry

    lax.fori_loop(0, base, finish_rows, 0)
    lax.fori_loop(0, base, finish_parts, 0)
    if base < chunks:
        lax.fori_loop(base, chunks, finish_large, 0)

        @pl.when(is_large)
        def _():
            lax.fori_loop(base, chunks, finish_parts, 0)


def kernel_device(
    base, large, variant, new_rows, counts, history_len, user_owner, cache_kv, w_out
):
    dp_count = lax.axis_size("dp")
    mp_count = lax.axis_size("mp")
    width = w_out.shape[1]
    local_rows = new_rows.shape[0]
    history_cap = cache_kv.shape[1]
    chunks = CAP // (dp_count * TILE)
    chunk = dp_count * TILE
    smem = pl.BlockSpec(memory_space=pltpu.SMEM)
    vmem = pl.BlockSpec(memory_space=pltpu.VMEM)
    dma = pltpu.SemaphoreType.DMA
    key_value, results = pl.pallas_call(
        functools.partial(layer_kernel, dp_count, mp_count, min(base, chunks), large),
        out_shape=(
            jax.ShapeDtypeStruct((CAP, 2 * width), jnp.bfloat16),
            jax.ShapeDtypeStruct((CAP, width), jnp.bfloat16),
        ),
        in_specs=[smem, smem, smem, vmem, vmem, pl.BlockSpec(memory_space=pltpu.HBM)],
        out_specs=(vmem, vmem),
        scratch_shapes=[
            pltpu.VMEM(w_out.shape, jnp.bfloat16),
            pltpu.VMEM((chunks, dp_count, TILE, 4 * width), jnp.bfloat16),
            pltpu.VMEM((chunks, dp_count, TILE, 4 * width), jnp.bfloat16),
            pltpu.VMEM((width, history_cap), jnp.bfloat16),
            pltpu.VMEM((history_cap, width), jnp.bfloat16),
            pltpu.VMEM((chunk, chunk), jnp.bfloat16),
            pltpu.VMEM((chunk, width), jnp.float32),
            pltpu.VMEM((chunk, width), jnp.float32),
            pltpu.VMEM((chunks, mp_count, 8, chunk), jnp.float32),
            pltpu.VMEM((chunks, mp_count, chunk, width), jnp.bfloat16),
            dma((chunks, dp_count)),
            dma((chunks, dp_count)),
            dma((chunks, mp_count)),
            dma((chunks, mp_count)),
            dma((chunks, mp_count)),
            dma((chunks, mp_count)),
            dma,
        ],
        compiler_params=pltpu.CompilerParams(
            collective_id=variant, has_side_effects=True, vmem_limit_bytes=40 * 2**20
        ),
    )(
        counts,
        history_len,
        user_owner,
        new_rows.reshape(local_rows, 4 * width),
        cache_kv.reshape(history_cap, 2 * width),
        w_out,
    )
    return (key_value.reshape(1, CAP, 2, width), results[None])


def switched_device(new_rows, counts, history_len, user_owner, cache_kv, w_out):
    dp_count = lax.axis_size("dp")
    half = dp_count // 2
    base = 3
    pairs = list(itertools.combinations(range(half), 2))
    branches = [
        functools.partial(kernel_device, base, (a, b, a + half, b + half), variant)
        for variant, (a, b) in enumerate(pairs)
    ]
    branches.append(
        functools.partial(kernel_device, CAP, tuple(range(dp_count)), len(pairs))
    )
    over = counts > base * dp_count * TILE
    places = lax.reduce(
        jnp.where(over, jnp.left_shift(1, user_owner % half), 0).astype(jnp.int32),
        jnp.int32(0),
        lax.bitwise_or,
        (0,),
    )
    choice = jnp.int32(len(pairs))
    for variant, (a, b) in enumerate(pairs):
        outside = places & jnp.int32((1 << half) - 1 - (1 << a) - (1 << b))
        choice = jnp.where(outside == 0, jnp.int32(variant), choice)
    return lax.switch(
        choice, branches, new_rows, counts, history_len, user_owner, cache_kv, w_out
    )


def solution(mesh):
    placed = (P(None, "dp", None, "mp"), P(), P(), P(), P("dp", None, None, "mp"), P(None, "mp"))
    fits = mesh.shape["dp"] * TILE == 128
    return jax.shard_map(
        switched_device if fits else general_device,
        mesh=mesh,
        in_specs=placed,
        out_specs=(P("dp", None, None, "mp"), P("dp", None, "mp")),
        check_vma=False,
    )
```

```python
import functools
import math

import jax
import jax.numpy as jnp
from jax import lax
from jax.experimental import pallas as pl
from jax.experimental.pallas import tpu as pltpu
from jax.sharding import PartitionSpec as P

DH = 128
CAP = 640
TILE = 16


EPSILON = 1e-06


def normalize(attended, gate_rows, width_all):
    total_sum, total_squares = lax.psum(
        (jnp.sum(attended, axis=-1), jnp.sum(attended * attended, axis=-1)), "mp"
    )
    row_mean = total_sum / width_all
    row_var = total_squares / width_all - row_mean * row_mean
    normed = (attended - row_mean[:, None]) * lax.rsqrt(row_var + EPSILON)[:, None]
    return (normed * gate_rows.astype(jnp.float32)).astype(jnp.bfloat16)


def project(gated, w_out):
    return jnp.dot(
        lax.all_gather(gated, "mp", axis=1, tiled=True), w_out, preferred_element_type=jnp.float32
    )


def general_device(new_rows, counts, history_len, user_owner, cache_kv, w_out):
    dp_count = lax.axis_size("dp")
    my_index = lax.axis_index("dp")
    local_rows = new_rows.shape[0]
    per_peer = CAP // dp_count
    width_all = w_out.shape[0]
    user_ids = jnp.arange(counts.shape[0], dtype=jnp.int32)
    starts = jnp.cumsum(counts) - counts
    event_ids = jnp.arange(local_rows, dtype=jnp.int32) * dp_count + my_index
    row_user = jnp.sum((starts[None, :] <= event_ids[:, None]).astype(jnp.int32), axis=1) - 1
    one_hot = (user_ids[None, :] == row_user[:, None]).astype(jnp.int32)
    row_first = jnp.sum(one_hot * starts[None, :], axis=1)
    row_owner = jnp.sum(one_hot * user_owner[None, :], axis=1)
    position = (event_ids - row_first) // dp_count * dp_count + row_owner
    is_mine = (user_owner == my_index).astype(jnp.int32)
    new_count = jnp.sum(counts * is_mine)
    first_row = jnp.sum(starts * is_mine)
    history = jnp.sum(history_len * is_mine)
    is_live = jnp.arange(CAP, dtype=jnp.int32) < new_count
    event_rows = new_rows[:, 0]
    feature_here = event_rows.shape[-1]
    heads_here = feature_here // DH
    history_cap = cache_kv.shape[1]
    cache_keys = cache_kv[0, :, 0].reshape(history_cap, heads_here, DH)
    cache_values = cache_kv[0, :, 1].reshape(history_cap, heads_here, DH)
    score_scale = 1.0 / math.sqrt(DH)
    buffer = jnp.zeros((CAP,) + event_rows.shape[1:], event_rows.dtype).at[position].set(event_rows)
    arrived = lax.all_to_all(
        buffer.reshape((per_peer, dp_count) + event_rows.shape[1:]),
        "dp",
        split_axis=1,
        concat_axis=1,
        tiled=True,
    )
    ordered = jnp.roll(arrived, -first_row, axis=1).reshape((CAP,) + arrived.shape[2:])
    queries = ordered[:, 0].reshape(CAP, heads_here, DH)
    own_keys = ordered[:, 1].reshape(CAP, heads_here, DH)
    own_values = ordered[:, 2].reshape(CAP, heads_here, DH)
    scores = (
        jnp.einsum("ehd,jhd->hej", queries, cache_keys, preferred_element_type=jnp.float32)
        * score_scale
    )
    visible = jnp.arange(history_cap, dtype=jnp.int32) < history
    weights = jnp.where(visible[None, None, :], jax.nn.silu(scores), 0.0).astype(jnp.bfloat16)
    summed = jnp.einsum("hej,jhd->ehd", weights, cache_values, preferred_element_type=jnp.float32)
    own_score = (
        jnp.sum(queries.astype(jnp.float32) * own_keys.astype(jnp.float32), axis=-1) * score_scale
    )
    attended = (summed + jax.nn.silu(own_score)[:, :, None] * own_values.astype(jnp.float32)) / (
        history + 1
    ).astype(jnp.float32)
    attended = attended.reshape(CAP, feature_here)
    gated = normalize(attended, ordered[:, 3], width_all)
    mixed_rows = project(gated, w_out)
    results = jnp.where(is_live[:, None], mixed_rows, 0.0).astype(jnp.bfloat16)
    key_value = ordered[:, 1:3]
    return (key_value[None], results[None])


def half_silu(half):
    return half + half * jnp.tanh(half)


def layer_kernel(
    dp_count,
    mp_count,
    base,
    large,
    counts_ref,
    history_ref,
    owner_ref,
    rows_ref,
    cache_ref,
    w_ref,
    kv_ref,
    out_ref,
    w_buf,
    send_buf,
    recv_buf,
    keys_buf,
    values_buf,
    perm_buf,
    attended_buf,
    gate_buf,
    stats_buf,
    gated_buf,
    row_send,
    row_recv,
    stats_send,
    stats_recv,
    gated_send,
    gated_recv,
    w_sem,
):
    fetch_w = pltpu.make_async_copy(w_ref, w_buf, w_sem)
    fetch_w.start()
    me = lax.axis_index("dp")
    my_part = lax.axis_index("mp")
    users = counts_ref.shape[0]
    local_rows = rows_ref.shape[0]
    width = w_ref.shape[1]
    width_all = w_ref.shape[0]
    heads = width // DH
    history_cap = cache_ref.shape[0]
    chunks = send_buf.shape[0]
    chunk = dp_count * TILE
    half_scale = 0.5 / math.sqrt(DH)
    is_large = functools.reduce(jnp.logical_or, [me == slot for slot in large])

    def peer(step):
        return lax.rem(me + step, dp_count)

    def part(step):
        return lax.rem(my_part + step, mp_count)

    def row_copy(c, source, target):
        return pltpu.make_async_remote_copy(
            src_ref=send_buf.at[c, target],
            dst_ref=recv_buf.at[c, source],
            send_sem=row_send.at[c, target],
            recv_sem=row_recv.at[c, source],
            device_id=(target, my_part),
            device_id_type=pl.DeviceIdType.MESH,
        )

    def part_copy(buf, send_sem, recv_sem, c, source, target):
        return pltpu.make_async_remote_copy(
            src_ref=buf.at[c, source],
            dst_ref=buf.at[c, source],
            send_sem=send_sem.at[c, target],
            recv_sem=recv_sem.at[c, source],
            device_id=(me, target),
            device_id_type=pl.DeviceIdType.MESH,
        )

    barrier = pltpu.get_barrier_semaphore()
    for step in range(1, dp_count):
        pl.semaphore_signal(
            barrier, inc=1, device_id=(peer(step), my_part), device_id_type=pl.DeviceIdType.MESH
        )
    for step in range(1, mp_count):
        pl.semaphore_signal(
            barrier, inc=1, device_id=(me, part(step)), device_id_type=pl.DeviceIdType.MESH
        )

    slot_first = [jnp.int32(0)] * dp_count
    my_count = jnp.int32(0)
    my_first = jnp.int32(0)
    my_history = jnp.int32(0)
    first = jnp.int32(0)
    for user in range(users):
        count = counts_ref[user]
        owner = owner_ref[user]
        slot_first = [
            jnp.where(owner == slot, first, slot_first[slot]) for slot in range(dp_count)
        ]
        mine = owner == me
        my_count = jnp.where(mine, count, my_count)
        my_first = jnp.where(mine, first, my_first)
        my_history = jnp.where(mine, history_ref[user], my_history)
        first = first + count
    slot_row = [lax.div(value - me + (dp_count - 1), dp_count) for value in slot_first]

    row_id = lax.broadcasted_iota(jnp.int32, (TILE, local_rows), 1)
    tile_id = lax.broadcasted_iota(jnp.int32, (TILE, local_rows), 0)
    offset = row_id - tile_id

    def pack(c, slots):
        picked = jnp.concatenate(
            [
                jnp.where(offset == slot_row[slot] + c * TILE, 1.0, 0.0).astype(jnp.bfloat16)
                for slot in slots
            ],
            axis=0,
        )
        sent = jnp.dot(picked, rows_ref[...], preferred_element_type=jnp.float32)
        return sent.astype(jnp.bfloat16).reshape(len(slots), TILE, 4 * width)

    def pack_into(c):
        @pl.when(c < base)
        def _():
            send_buf[c] = pack(c, range(dp_count))

        if base < chunks:

            @pl.when(jnp.logical_and(c >= base, c < chunks))
            def _():
                sent = pack(c, large)
                for index, slot in enumerate(large):
                    send_buf[c, slot] = sent[index]

    def each_copy(c, act):
        @pl.when(c < base)
        def _():
            for step in range(1, dp_count):
                act(row_copy(c, me, peer(step)))

        if base < chunks:

            @pl.when(jnp.logical_and(c >= base, c < chunks))
            def _():
                for slot in large:

                    @pl.when(me != slot)
                    def _():
                        act(row_copy(c, me, slot))

    def post(c):
        each_copy(c, lambda copy: copy.start())

    pack_into(0)
    pl.semaphore_wait(barrier, dp_count - 1 + mp_count - 1)
    post(0)
    pack_into(1)
    post(1)
    pack_into(2)

    place = lax.broadcasted_iota(jnp.int32, (chunk, chunk), 0)
    landed = lax.broadcasted_iota(jnp.int32, (chunk, chunk), 1)
    source_of = landed // TILE
    ordered_at = dp_count * (landed - source_of * TILE) + lax.rem(
        source_of - lax.rem(my_first, dp_count) + dp_count, dp_count
    )
    perm_buf[...] = jnp.where(place == ordered_at, 1.0, 0.0).astype(jnp.bfloat16)
    keys_buf[...] = cache_ref[:, :width].astype(jnp.float32).T.astype(jnp.bfloat16)
    history_id = lax.broadcasted_iota(jnp.int32, (history_cap, width), 0)
    values_buf[...] = jnp.where(
        history_id < my_history, cache_ref[:, width:].astype(jnp.float32), 0.0
    ).astype(jnp.bfloat16)
    line = lax.broadcasted_iota(jnp.int32, (8, chunk), 0)
    chunk_row = lax.broadcasted_iota(jnp.int32, (chunk, 1), 0)
    inverse = 1.0 / (my_history + 1).astype(jnp.float32)

    def attend(c):
        recv_buf[c, me] = send_buf[c, me]
        for step in range(1, dp_count):
            row_copy(c, peer(step), me).wait_recv()
        arrived = recv_buf[c].reshape(chunk, 4 * width)
        ordered = jnp.dot(perm_buf[...], arrived, preferred_element_type=jnp.float32)
        here = pl.ds(pl.multiple_of(c * chunk, chunk), chunk)
        live = c * chunk + chunk_row < my_count
        kv_ref[here, :] = jnp.where(live, ordered[:, width : 3 * width], 0.0).astype(jnp.bfloat16)
        gate_buf[...] = ordered[:, 3 * width :]
        total = jnp.zeros((chunk, DH), jnp.float32)
        squares = jnp.zeros((chunk, DH), jnp.float32)
        for head in range(heads):
            columns = slice(head * DH, (head + 1) * DH)
            query = ordered[:, columns]
            key = ordered[:, width + head * DH : width + (head + 1) * DH]
            value = ordered[:, 2 * width + head * DH : 2 * width + (head + 1) * DH]
            half = (
                jnp.dot(
                    query.astype(jnp.bfloat16),
                    keys_buf[columns, :],
                    preferred_element_type=jnp.float32,
                )
                * half_scale
            )
            summed = jnp.dot(
                half_silu(half).astype(jnp.bfloat16),
                values_buf[:, columns],
                preferred_element_type=jnp.float32,
            )
            own = jnp.sum(query * key, axis=1, keepdims=True) * half_scale
            attended = (summed + half_silu(own) * value) * inverse
            attended_buf[:, columns] = attended
            total = total + attended
            squares = squares + attended * attended
        total = jnp.sum(total.T, axis=0, keepdims=True)
        squares = jnp.sum(squares.T, axis=0, keepdims=True)
        stats_buf[c, my_part] = jnp.where(line == 0, total, jnp.where(line == 1, squares, 0.0))
        for step in range(1, mp_count):
            part_copy(stats_buf, stats_send, stats_recv, c, my_part, part(step)).start()

    def gate(c):
        for step in range(1, mp_count):
            part_copy(stats_buf, stats_send, stats_recv, c, part(step), my_part).wait_recv()
        stats = stats_buf[c, 0]
        for index in range(1, mp_count):
            stats = stats + stats_buf[c, index]
        mean = stats[0:1] / width_all
        variance = stats[1:2] / width_all - mean * mean
        stats = jnp.where(line == 0, mean, lax.rsqrt(variance + EPSILON))
        stats = jnp.concatenate([stats, jnp.zeros((128 - 8, chunk), jnp.float32)], axis=0).T
        normed = (attended_buf[...] - stats[:, 0:1]) * stats[:, 1:2]
        gated_buf[c, my_part] = (normed * gate_buf[...]).astype(jnp.bfloat16)
        for step in range(1, mp_count):
            part_copy(gated_buf, gated_send, gated_recv, c, my_part, part(step)).start()

    def mix(c):
        for step in range(1, mp_count):
            part_copy(gated_buf, gated_send, gated_recv, c, part(step), my_part).wait_recv()
        mixed = jnp.zeros((chunk, width), jnp.float32)
        for index in range(mp_count):
            mixed = mixed + jnp.dot(
                gated_buf[c, index],
                w_buf[index * width : (index + 1) * width, :],
                preferred_element_type=jnp.float32,
            )
        here = pl.ds(pl.multiple_of(c * chunk, chunk), chunk)
        live = c * chunk + chunk_row < my_count
        out_ref[here, :] = jnp.where(live, mixed, 0.0).astype(jnp.bfloat16)

    def works(c):
        return jnp.logical_or(c < base, is_large)

    def step_of(c, carry):
        each_copy(c, lambda copy: copy.wait_send())
        post(c + 2)

        @pl.when(works(c))
        def _():
            attend(c)

        pack_into(c + 3)

        @pl.when(jnp.logical_and(c > 0, works(c - 1)))
        def _():
            mix(c - 1)

        @pl.when(works(c))
        def _():
            gate(c)

        return carry

    lax.fori_loop(0, 1, step_of, 0)
    fetch_w.wait()
    lax.fori_loop(1, chunks, step_of, 0)

    @pl.when(works(chunks - 1))
    def _():
        mix(chunks - 1)

    if base < chunks:

        @pl.when(jnp.logical_not(is_large))
        def _():
            kv_ref[base * chunk :, :] = jnp.zeros(
                ((chunks - base) * chunk, 2 * width), jnp.bfloat16
            )
            out_ref[base * chunk :, :] = jnp.zeros(((chunks - base) * chunk, width), jnp.bfloat16)

    def finish_parts(c, carry):
        for step in range(1, mp_count):
            part_copy(stats_buf, stats_send, stats_recv, c, my_part, part(step)).wait_send()
            part_copy(gated_buf, gated_send, gated_recv, c, my_part, part(step)).wait_send()
        return carry

    lax.fori_loop(0, base, finish_parts, 0)
    if base < chunks:

        @pl.when(is_large)
        def _():
            lax.fori_loop(base, chunks, finish_parts, 0)


def kernel_device(
    base, large, variant, new_rows, counts, history_len, user_owner, cache_kv, w_out
):
    dp_count = lax.axis_size("dp")
    mp_count = lax.axis_size("mp")
    width = w_out.shape[1]
    local_rows = new_rows.shape[0]
    history_cap = cache_kv.shape[1]
    chunks = CAP // (dp_count * TILE)
    chunk = dp_count * TILE
    smem = pl.BlockSpec(memory_space=pltpu.SMEM)
    vmem = pl.BlockSpec(memory_space=pltpu.VMEM)
    dma = pltpu.SemaphoreType.DMA
    key_value, results = pl.pallas_call(
        functools.partial(layer_kernel, dp_count, mp_count, min(base, chunks), large),
        out_shape=(
            jax.ShapeDtypeStruct((CAP, 2 * width), jnp.bfloat16),
            jax.ShapeDtypeStruct((CAP, width), jnp.bfloat16),
        ),
        in_specs=[smem, smem, smem, vmem, vmem, pl.BlockSpec(memory_space=pltpu.HBM)],
        out_specs=(vmem, vmem),
        scratch_shapes=[
            pltpu.VMEM(w_out.shape, jnp.bfloat16),
            pltpu.VMEM((chunks, dp_count, TILE, 4 * width), jnp.bfloat16),
            pltpu.VMEM((chunks, dp_count, TILE, 4 * width), jnp.bfloat16),
            pltpu.VMEM((width, history_cap), jnp.bfloat16),
            pltpu.VMEM((history_cap, width), jnp.bfloat16),
            pltpu.VMEM((chunk, chunk), jnp.bfloat16),
            pltpu.VMEM((chunk, width), jnp.float32),
            pltpu.VMEM((chunk, width), jnp.float32),
            pltpu.VMEM((chunks, mp_count, 8, chunk), jnp.float32),
            pltpu.VMEM((chunks, mp_count, chunk, width), jnp.bfloat16),
            dma((chunks, dp_count)),
            dma((chunks, dp_count)),
            dma((chunks, mp_count)),
            dma((chunks, mp_count)),
            dma((chunks, mp_count)),
            dma((chunks, mp_count)),
            dma,
        ],
        compiler_params=pltpu.CompilerParams(
            collective_id=variant, has_side_effects=True, vmem_limit_bytes=40 * 2**20
        ),
    )(
        counts,
        history_len,
        user_owner,
        new_rows.reshape(local_rows, 4 * width),
        cache_kv.reshape(history_cap, 2 * width),
        w_out,
    )
    return (key_value.reshape(1, CAP, 2, width), results[None])


def whole_device(*arrays):
    slots = tuple(range(lax.axis_size("dp")))
    return kernel_device(CAP, slots, 0, *arrays)


def solution(mesh):
    placed = (P(None, "dp", None, "mp"), P(), P(), P(), P("dp", None, None, "mp"), P(None, "mp"))
    fits = mesh.shape["dp"] * TILE == 128
    return jax.shard_map(
        whole_device if fits else general_device,
        mesh=mesh,
        in_specs=placed,
        out_specs=(P("dp", None, None, "mp"), P("dp", None, "mp")),
        check_vma=False,
    )
```

```python
import functools
import itertools
import math

import jax
import jax.numpy as jnp
from jax import lax
from jax.experimental import pallas as pl
from jax.experimental.pallas import tpu as pltpu
from jax.sharding import PartitionSpec as P

DH = 128
CAP = 640
TILE = 16


EPSILON = 1e-06


def normalize(attended, gate_rows, width_all):
    total_sum, total_squares = lax.psum(
        (jnp.sum(attended, axis=-1), jnp.sum(attended * attended, axis=-1)), "mp"
    )
    row_mean = total_sum / width_all
    row_var = total_squares / width_all - row_mean * row_mean
    normed = (attended - row_mean[:, None]) * lax.rsqrt(row_var + EPSILON)[:, None]
    return (normed * gate_rows.astype(jnp.float32)).astype(jnp.bfloat16)


def project(gated, w_out):
    return jnp.dot(
        lax.all_gather(gated, "mp", axis=1, tiled=True), w_out, preferred_element_type=jnp.float32
    )


def general_device(new_rows, counts, history_len, user_owner, cache_kv, w_out):
    dp_count = lax.axis_size("dp")
    my_index = lax.axis_index("dp")
    local_rows = new_rows.shape[0]
    per_peer = CAP // dp_count
    width_all = w_out.shape[0]
    user_ids = jnp.arange(counts.shape[0], dtype=jnp.int32)
    starts = jnp.cumsum(counts) - counts
    event_ids = jnp.arange(local_rows, dtype=jnp.int32) * dp_count + my_index
    row_user = jnp.sum((starts[None, :] <= event_ids[:, None]).astype(jnp.int32), axis=1) - 1
    one_hot = (user_ids[None, :] == row_user[:, None]).astype(jnp.int32)
    row_first = jnp.sum(one_hot * starts[None, :], axis=1)
    row_owner = jnp.sum(one_hot * user_owner[None, :], axis=1)
    position = (event_ids - row_first) // dp_count * dp_count + row_owner
    is_mine = (user_owner == my_index).astype(jnp.int32)
    new_count = jnp.sum(counts * is_mine)
    first_row = jnp.sum(starts * is_mine)
    history = jnp.sum(history_len * is_mine)
    is_live = jnp.arange(CAP, dtype=jnp.int32) < new_count
    event_rows = new_rows[:, 0]
    feature_here = event_rows.shape[-1]
    heads_here = feature_here // DH
    history_cap = cache_kv.shape[1]
    cache_keys = cache_kv[0, :, 0].reshape(history_cap, heads_here, DH)
    cache_values = cache_kv[0, :, 1].reshape(history_cap, heads_here, DH)
    score_scale = 1.0 / math.sqrt(DH)
    buffer = jnp.zeros((CAP,) + event_rows.shape[1:], event_rows.dtype).at[position].set(event_rows)
    arrived = lax.all_to_all(
        buffer.reshape((per_peer, dp_count) + event_rows.shape[1:]),
        "dp",
        split_axis=1,
        concat_axis=1,
        tiled=True,
    )
    ordered = jnp.roll(arrived, -first_row, axis=1).reshape((CAP,) + arrived.shape[2:])
    queries = ordered[:, 0].reshape(CAP, heads_here, DH)
    own_keys = ordered[:, 1].reshape(CAP, heads_here, DH)
    own_values = ordered[:, 2].reshape(CAP, heads_here, DH)
    scores = (
        jnp.einsum("ehd,jhd->hej", queries, cache_keys, preferred_element_type=jnp.float32)
        * score_scale
    )
    visible = jnp.arange(history_cap, dtype=jnp.int32) < history
    weights = jnp.where(visible[None, None, :], jax.nn.silu(scores), 0.0).astype(jnp.bfloat16)
    summed = jnp.einsum("hej,jhd->ehd", weights, cache_values, preferred_element_type=jnp.float32)
    own_score = (
        jnp.sum(queries.astype(jnp.float32) * own_keys.astype(jnp.float32), axis=-1) * score_scale
    )
    attended = (summed + jax.nn.silu(own_score)[:, :, None] * own_values.astype(jnp.float32)) / (
        history + 1
    ).astype(jnp.float32)
    attended = attended.reshape(CAP, feature_here)
    gated = normalize(attended, ordered[:, 3], width_all)
    mixed_rows = project(gated, w_out)
    results = jnp.where(is_live[:, None], mixed_rows, 0.0).astype(jnp.bfloat16)
    key_value = ordered[:, 1:3]
    return (key_value[None], results[None])


def half_silu(half):
    return half + half * jnp.tanh(half)


def layer_kernel(
    dp_count,
    mp_count,
    low,
    high,
    large,
    counts_ref,
    history_ref,
    owner_ref,
    rows_ref,
    cache_ref,
    w_ref,
    kv_ref,
    out_ref,
    w_buf,
    send_buf,
    recv_buf,
    keys_buf,
    values_buf,
    perm_buf,
    attended_buf,
    gate_buf,
    stats_buf,
    gated_buf,
    row_send,
    row_recv,
    stats_send,
    stats_recv,
    gated_send,
    gated_recv,
    w_sem,
):
    fetch_w = pltpu.make_async_copy(w_ref, w_buf, w_sem)
    fetch_w.start()
    me = lax.axis_index("dp")
    my_part = lax.axis_index("mp")
    users = counts_ref.shape[0]
    local_rows = rows_ref.shape[0]
    width = w_ref.shape[1]
    width_all = w_ref.shape[0]
    heads = width // DH
    history_cap = cache_ref.shape[0]
    chunks = send_buf.shape[0]
    chunk = dp_count * TILE
    half_scale = 0.5 / math.sqrt(DH)
    is_large = functools.reduce(jnp.logical_or, [me == slot for slot in large])

    def peer(step):
        return lax.rem(me + step, dp_count)

    def part(step):
        return lax.rem(my_part + step, mp_count)

    def row_copy(c, source, target):
        return pltpu.make_async_remote_copy(
            src_ref=send_buf.at[c, target],
            dst_ref=recv_buf.at[c, source],
            send_sem=row_send.at[c, target],
            recv_sem=row_recv.at[c, source],
            device_id=(target, my_part),
            device_id_type=pl.DeviceIdType.MESH,
        )

    def part_copy(buf, send_sem, recv_sem, c, source, target):
        return pltpu.make_async_remote_copy(
            src_ref=buf.at[c, source],
            dst_ref=buf.at[c, source],
            send_sem=send_sem.at[c, target],
            recv_sem=recv_sem.at[c, source],
            device_id=(me, target),
            device_id_type=pl.DeviceIdType.MESH,
        )

    barrier = pltpu.get_barrier_semaphore()
    for step in range(1, dp_count):
        pl.semaphore_signal(
            barrier, inc=1, device_id=(peer(step), my_part), device_id_type=pl.DeviceIdType.MESH
        )
    for step in range(1, mp_count):
        pl.semaphore_signal(
            barrier, inc=1, device_id=(me, part(step)), device_id_type=pl.DeviceIdType.MESH
        )

    slot_first = [jnp.int32(0)] * dp_count
    my_count = jnp.int32(0)
    my_first = jnp.int32(0)
    my_history = jnp.int32(0)
    first = jnp.int32(0)
    for user in range(users):
        count = counts_ref[user]
        owner = owner_ref[user]
        slot_first = [
            jnp.where(owner == slot, first, slot_first[slot]) for slot in range(dp_count)
        ]
        mine = owner == me
        my_count = jnp.where(mine, count, my_count)
        my_first = jnp.where(mine, first, my_first)
        my_history = jnp.where(mine, history_ref[user], my_history)
        first = first + count
    slot_row = [
        lax.div(value - me + (dp_count - 1), dp_count) - (0 if slot in large else low * TILE)
        for slot, value in enumerate(slot_first)
    ]
    first_step = jnp.where(is_large, 0, low)

    row_id = lax.broadcasted_iota(jnp.int32, (TILE, local_rows), 1)
    tile_id = lax.broadcasted_iota(jnp.int32, (TILE, local_rows), 0)
    offset = row_id - tile_id

    def pack(c, slots):
        picked = jnp.concatenate(
            [
                jnp.where(offset == slot_row[slot] + c * TILE, 1.0, 0.0).astype(jnp.bfloat16)
                for slot in slots
            ],
            axis=0,
        )
        sent = jnp.dot(picked, rows_ref[...], preferred_element_type=jnp.float32)
        return sent.astype(jnp.bfloat16).reshape(len(slots), TILE, 4 * width)

    def for_all(c):
        return jnp.logical_and(c >= low, c < high)

    def for_large(c):
        return jnp.logical_or(c < low, jnp.logical_and(c >= high, c < chunks))

    def pack_into(c):
        @pl.when(for_all(c))
        def _():
            send_buf[c] = pack(c, range(dp_count))

        if high - low < chunks:

            @pl.when(for_large(c))
            def _():
                sent = pack(c, large)
                for index, slot in enumerate(large):
                    send_buf[c, slot] = sent[index]

    def each_copy(c, act):
        @pl.when(for_all(c))
        def _():
            for step in range(1, dp_count):
                act(row_copy(c, me, peer(step)))

        if high - low < chunks:

            @pl.when(for_large(c))
            def _():
                for slot in large:

                    @pl.when(me != slot)
                    def _():
                        act(row_copy(c, me, slot))

    def post(c):
        each_copy(c, lambda copy: copy.start())

    pack_into(0)
    pl.semaphore_wait(barrier, dp_count - 1 + mp_count - 1)
    post(0)
    pack_into(1)
    post(1)
    pack_into(2)

    place = lax.broadcasted_iota(jnp.int32, (chunk, chunk), 0)
    landed = lax.broadcasted_iota(jnp.int32, (chunk, chunk), 1)
    source_of = landed // TILE
    ordered_at = dp_count * (landed - source_of * TILE) + lax.rem(
        source_of - lax.rem(my_first, dp_count) + dp_count, dp_count
    )
    perm_buf[...] = jnp.where(place == ordered_at, 1.0, 0.0).astype(jnp.bfloat16)
    keys_buf[...] = cache_ref[:, :width].astype(jnp.float32).T.astype(jnp.bfloat16)
    history_id = lax.broadcasted_iota(jnp.int32, (history_cap, width), 0)
    values_buf[...] = jnp.where(
        history_id < my_history, cache_ref[:, width:].astype(jnp.float32), 0.0
    ).astype(jnp.bfloat16)
    line = lax.broadcasted_iota(jnp.int32, (8, chunk), 0)
    chunk_row = lax.broadcasted_iota(jnp.int32, (chunk, 1), 0)
    inverse = 1.0 / (my_history + 1).astype(jnp.float32)

    def attend(c):
        recv_buf[c, me] = send_buf[c, me]
        for step in range(1, dp_count):
            row_copy(c, peer(step), me).wait_recv()
        arrived = recv_buf[c].reshape(chunk, 4 * width)
        ordered = jnp.dot(perm_buf[...], arrived, preferred_element_type=jnp.float32)
        here = pl.ds(pl.multiple_of((c - first_step) * chunk, chunk), chunk)
        live = (c - first_step) * chunk + chunk_row < my_count
        kv_ref[here, :] = jnp.where(live, ordered[:, width : 3 * width], 0.0).astype(jnp.bfloat16)
        gate_buf[...] = ordered[:, 3 * width :]
        total = jnp.zeros((chunk, DH), jnp.float32)
        squares = jnp.zeros((chunk, DH), jnp.float32)
        for head in range(heads):
            columns = slice(head * DH, (head + 1) * DH)
            query = ordered[:, columns]
            key = ordered[:, width + head * DH : width + (head + 1) * DH]
            value = ordered[:, 2 * width + head * DH : 2 * width + (head + 1) * DH]
            half = (
                jnp.dot(
                    query.astype(jnp.bfloat16),
                    keys_buf[columns, :],
                    preferred_element_type=jnp.float32,
                )
                * half_scale
            )
            summed = jnp.dot(
                half_silu(half).astype(jnp.bfloat16),
                values_buf[:, columns],
                preferred_element_type=jnp.float32,
            )
            own = jnp.sum(query * key, axis=1, keepdims=True) * half_scale
            attended = (summed + half_silu(own) * value) * inverse
            attended_buf[:, columns] = attended
            total = total + attended
            squares = squares + attended * attended
        total = jnp.sum(total.T, axis=0, keepdims=True)
        squares = jnp.sum(squares.T, axis=0, keepdims=True)
        stats_buf[c, my_part] = jnp.where(line == 0, total, jnp.where(line == 1, squares, 0.0))
        for step in range(1, mp_count):
            part_copy(stats_buf, stats_send, stats_recv, c, my_part, part(step)).start()

    def gate(c):
        for step in range(1, mp_count):
            part_copy(stats_buf, stats_send, stats_recv, c, part(step), my_part).wait_recv()
        stats = stats_buf[c, 0]
        for index in range(1, mp_count):
            stats = stats + stats_buf[c, index]
        mean = stats[0:1] / width_all
        variance = stats[1:2] / width_all - mean * mean
        stats = jnp.where(line == 0, mean, lax.rsqrt(variance + EPSILON))
        stats = jnp.concatenate([stats, jnp.zeros((128 - 8, chunk), jnp.float32)], axis=0).T
        normed = (attended_buf[...] - stats[:, 0:1]) * stats[:, 1:2]
        gated_buf[c, my_part] = (normed * gate_buf[...]).astype(jnp.bfloat16)
        for step in range(1, mp_count):
            part_copy(gated_buf, gated_send, gated_recv, c, my_part, part(step)).start()

    def mix(c):
        for step in range(1, mp_count):
            part_copy(gated_buf, gated_send, gated_recv, c, part(step), my_part).wait_recv()
        mixed = jnp.zeros((chunk, width), jnp.float32)
        for index in range(mp_count):
            mixed = mixed + jnp.dot(
                gated_buf[c, index],
                w_buf[index * width : (index + 1) * width, :],
                preferred_element_type=jnp.float32,
            )
        here = pl.ds(pl.multiple_of((c - first_step) * chunk, chunk), chunk)
        live = (c - first_step) * chunk + chunk_row < my_count
        out_ref[here, :] = jnp.where(live, mixed, 0.0).astype(jnp.bfloat16)

    def works(c):
        return jnp.logical_or(is_large, for_all(c))

    def step_of(c, carry):
        each_copy(c, lambda copy: copy.wait_send())
        post(c + 2)

        @pl.when(works(c))
        def _():
            attend(c)

        pack_into(c + 3)

        @pl.when(jnp.logical_and(c > 0, works(c - 1)))
        def _():
            mix(c - 1)

        @pl.when(works(c))
        def _():
            gate(c)

        return carry

    lax.fori_loop(0, 1, step_of, 0)
    fetch_w.wait()
    lax.fori_loop(1, chunks, step_of, 0)

    @pl.when(works(chunks - 1))
    def _():
        mix(chunks - 1)

    if high - low < chunks:
        rest = chunks - (high - low)

        @pl.when(jnp.logical_not(is_large))
        def _():
            kv_ref[(high - low) * chunk :, :] = jnp.zeros((rest * chunk, 2 * width), jnp.bfloat16)
            out_ref[(high - low) * chunk :, :] = jnp.zeros((rest * chunk, width), jnp.bfloat16)

    def finish_parts(c, carry):
        for step in range(1, mp_count):
            part_copy(stats_buf, stats_send, stats_recv, c, my_part, part(step)).wait_send()
            part_copy(gated_buf, gated_send, gated_recv, c, my_part, part(step)).wait_send()
        return carry

    lax.fori_loop(low, high, finish_parts, 0)
    if high - low < chunks:

        @pl.when(is_large)
        def _():
            lax.fori_loop(0, low, finish_parts, 0)
            lax.fori_loop(high, chunks, finish_parts, 0)


def kernel_device(
    low, high, large, variant, new_rows, counts, history_len, user_owner, cache_kv, w_out
):
    dp_count = lax.axis_size("dp")
    mp_count = lax.axis_size("mp")
    width = w_out.shape[1]
    local_rows = new_rows.shape[0]
    history_cap = cache_kv.shape[1]
    chunks = CAP // (dp_count * TILE)
    chunk = dp_count * TILE
    smem = pl.BlockSpec(memory_space=pltpu.SMEM)
    vmem = pl.BlockSpec(memory_space=pltpu.VMEM)
    dma = pltpu.SemaphoreType.DMA
    key_value, results = pl.pallas_call(
        functools.partial(layer_kernel, dp_count, mp_count, low, high, large),
        out_shape=(
            jax.ShapeDtypeStruct((CAP, 2 * width), jnp.bfloat16),
            jax.ShapeDtypeStruct((CAP, width), jnp.bfloat16),
        ),
        in_specs=[smem, smem, smem, vmem, vmem, pl.BlockSpec(memory_space=pltpu.HBM)],
        out_specs=(vmem, vmem),
        scratch_shapes=[
            pltpu.VMEM(w_out.shape, jnp.bfloat16),
            pltpu.VMEM((chunks, dp_count, TILE, 4 * width), jnp.bfloat16),
            pltpu.VMEM((chunks, dp_count, TILE, 4 * width), jnp.bfloat16),
            pltpu.VMEM((width, history_cap), jnp.bfloat16),
            pltpu.VMEM((history_cap, width), jnp.bfloat16),
            pltpu.VMEM((chunk, chunk), jnp.bfloat16),
            pltpu.VMEM((chunk, width), jnp.float32),
            pltpu.VMEM((chunk, width), jnp.float32),
            pltpu.VMEM((chunks, mp_count, 8, chunk), jnp.float32),
            pltpu.VMEM((chunks, mp_count, chunk, width), jnp.bfloat16),
            dma((chunks, dp_count)),
            dma((chunks, dp_count)),
            dma((chunks, mp_count)),
            dma((chunks, mp_count)),
            dma((chunks, mp_count)),
            dma((chunks, mp_count)),
            dma,
        ],
        compiler_params=pltpu.CompilerParams(
            collective_id=variant, has_side_effects=True, vmem_limit_bytes=40 * 2**20
        ),
    )(
        counts,
        history_len,
        user_owner,
        new_rows.reshape(local_rows, 4 * width),
        cache_kv.reshape(history_cap, 2 * width),
        w_out,
    )
    return (key_value.reshape(1, CAP, 2, width), results[None])


def switched_device(new_rows, counts, history_len, user_owner, cache_kv, w_out):
    dp_count = lax.axis_size("dp")
    chunks = CAP // (dp_count * TILE)
    half = dp_count // 2
    low, high = 1, 4
    pairs = list(itertools.combinations(range(half), 2))
    branches = [
        functools.partial(kernel_device, low, high, (a, b, a + half, b + half), variant)
        for variant, (a, b) in enumerate(pairs)
    ]
    branches.append(
        functools.partial(kernel_device, 0, chunks, tuple(range(dp_count)), len(pairs))
    )
    sets = jnp.array([[(1 << a) | (1 << b)] for a, b in pairs], jnp.int32)
    place = jnp.left_shift(1, user_owner % half)[None, :]
    over = (counts > (high - low) * dp_count * TILE)[None, :]
    misfits = jnp.sum(jnp.where(over & ((place & sets) == 0), 1, 0), axis=1)
    order = jnp.arange(len(pairs), dtype=jnp.int32)
    choice = jnp.min(jnp.where(misfits == 0, order, len(pairs)))
    return lax.switch(
        choice, branches, new_rows, counts, history_len, user_owner, cache_kv, w_out
    )


def solution(mesh):
    placed = (P(None, "dp", None, "mp"), P(), P(), P(), P("dp", None, None, "mp"), P(None, "mp"))
    fits = mesh.shape["dp"] * TILE == 128
    return jax.shard_map(
        switched_device if fits else general_device,
        mesh=mesh,
        in_specs=placed,
        out_specs=(P("dp", None, None, "mp"), P("dp", None, "mp")),
        check_vma=False,
    )
```

```python
import functools
import itertools
import math

import jax
import jax.numpy as jnp
from jax import lax
from jax.experimental import pallas as pl
from jax.experimental.pallas import tpu as pltpu
from jax.sharding import PartitionSpec as P

DH = 128
CAP = 640
TILE = 16


EPSILON = 1e-06


def normalize(attended, gate_rows, width_all):
    total_sum, total_squares = lax.psum(
        (jnp.sum(attended, axis=-1), jnp.sum(attended * attended, axis=-1)), "mp"
    )
    row_mean = total_sum / width_all
    row_var = total_squares / width_all - row_mean * row_mean
    normed = (attended - row_mean[:, None]) * lax.rsqrt(row_var + EPSILON)[:, None]
    return (normed * gate_rows.astype(jnp.float32)).astype(jnp.bfloat16)


def project(gated, w_out):
    return jnp.dot(
        lax.all_gather(gated, "mp", axis=1, tiled=True), w_out, preferred_element_type=jnp.float32
    )


def general_device(new_rows, counts, history_len, user_owner, cache_kv, w_out):
    dp_count = lax.axis_size("dp")
    my_index = lax.axis_index("dp")
    local_rows = new_rows.shape[0]
    per_peer = CAP // dp_count
    width_all = w_out.shape[0]
    user_ids = jnp.arange(counts.shape[0], dtype=jnp.int32)
    starts = jnp.cumsum(counts) - counts
    event_ids = jnp.arange(local_rows, dtype=jnp.int32) * dp_count + my_index
    row_user = jnp.sum((starts[None, :] <= event_ids[:, None]).astype(jnp.int32), axis=1) - 1
    one_hot = (user_ids[None, :] == row_user[:, None]).astype(jnp.int32)
    row_first = jnp.sum(one_hot * starts[None, :], axis=1)
    row_owner = jnp.sum(one_hot * user_owner[None, :], axis=1)
    position = (event_ids - row_first) // dp_count * dp_count + row_owner
    is_mine = (user_owner == my_index).astype(jnp.int32)
    new_count = jnp.sum(counts * is_mine)
    first_row = jnp.sum(starts * is_mine)
    history = jnp.sum(history_len * is_mine)
    is_live = jnp.arange(CAP, dtype=jnp.int32) < new_count
    event_rows = new_rows[:, 0]
    feature_here = event_rows.shape[-1]
    heads_here = feature_here // DH
    history_cap = cache_kv.shape[1]
    cache_keys = cache_kv[0, :, 0].reshape(history_cap, heads_here, DH)
    cache_values = cache_kv[0, :, 1].reshape(history_cap, heads_here, DH)
    score_scale = 1.0 / math.sqrt(DH)
    buffer = jnp.zeros((CAP,) + event_rows.shape[1:], event_rows.dtype).at[position].set(event_rows)
    arrived = lax.all_to_all(
        buffer.reshape((per_peer, dp_count) + event_rows.shape[1:]),
        "dp",
        split_axis=1,
        concat_axis=1,
        tiled=True,
    )
    ordered = jnp.roll(arrived, -first_row, axis=1).reshape((CAP,) + arrived.shape[2:])
    queries = ordered[:, 0].reshape(CAP, heads_here, DH)
    own_keys = ordered[:, 1].reshape(CAP, heads_here, DH)
    own_values = ordered[:, 2].reshape(CAP, heads_here, DH)
    scores = (
        jnp.einsum("ehd,jhd->hej", queries, cache_keys, preferred_element_type=jnp.float32)
        * score_scale
    )
    visible = jnp.arange(history_cap, dtype=jnp.int32) < history
    weights = jnp.where(visible[None, None, :], jax.nn.silu(scores), 0.0).astype(jnp.bfloat16)
    summed = jnp.einsum("hej,jhd->ehd", weights, cache_values, preferred_element_type=jnp.float32)
    own_score = (
        jnp.sum(queries.astype(jnp.float32) * own_keys.astype(jnp.float32), axis=-1) * score_scale
    )
    attended = (summed + jax.nn.silu(own_score)[:, :, None] * own_values.astype(jnp.float32)) / (
        history + 1
    ).astype(jnp.float32)
    attended = attended.reshape(CAP, feature_here)
    gated = normalize(attended, ordered[:, 3], width_all)
    mixed_rows = project(gated, w_out)
    results = jnp.where(is_live[:, None], mixed_rows, 0.0).astype(jnp.bfloat16)
    key_value = ordered[:, 1:3]
    return (key_value[None], results[None])


def half_silu(half):
    return half + half * jnp.tanh(half)


def layer_kernel(
    dp_count,
    mp_count,
    low,
    high,
    large,
    counts_ref,
    history_ref,
    owner_ref,
    rows_ref,
    cache_ref,
    w_ref,
    kv_ref,
    out_ref,
    w_buf,
    send_buf,
    recv_buf,
    keys_buf,
    values_buf,
    perm_buf,
    attended_buf,
    gate_buf,
    stats_buf,
    gated_buf,
    row_send,
    row_recv,
    stats_send,
    stats_recv,
    gated_send,
    gated_recv,
    w_sem,
):
    fetch_w = pltpu.make_async_copy(w_ref, w_buf, w_sem)
    fetch_w.start()
    me = lax.axis_index("dp")
    my_part = lax.axis_index("mp")
    users = counts_ref.shape[0]
    local_rows = rows_ref.shape[0]
    width = w_ref.shape[1]
    width_all = w_ref.shape[0]
    heads = width // DH
    history_cap = cache_ref.shape[0]
    chunks = send_buf.shape[0]
    chunk = dp_count * TILE
    half_scale = 0.5 / math.sqrt(DH)
    is_large = functools.reduce(jnp.logical_or, [me == slot for slot in large])

    def peer(step):
        return lax.rem(me + step, dp_count)

    def part(step):
        return lax.rem(my_part + step, mp_count)

    def row_copy(c, source, target):
        return pltpu.make_async_remote_copy(
            src_ref=send_buf.at[c, target],
            dst_ref=recv_buf.at[c, source],
            send_sem=row_send.at[c, target],
            recv_sem=row_recv.at[c, source],
            device_id=(target, my_part),
            device_id_type=pl.DeviceIdType.MESH,
        )

    def part_copy(buf, send_sem, recv_sem, c, source, target):
        return pltpu.make_async_remote_copy(
            src_ref=buf.at[c, source],
            dst_ref=buf.at[c, source],
            send_sem=send_sem.at[c, target],
            recv_sem=recv_sem.at[c, source],
            device_id=(me, target),
            device_id_type=pl.DeviceIdType.MESH,
        )

    my_core = lax.rem(my_part, 2)
    near = my_part + 1 - 2 * my_core
    far = lax.rem(my_part - my_core + 2, mp_count)

    def gated_copy(c, source, half, index, target):
        block = gated_buf.at[c, source] if half is None else gated_buf.at[c, source, half]
        return pltpu.make_async_remote_copy(
            src_ref=block,
            dst_ref=block,
            send_sem=gated_send.at[c, index],
            recv_sem=gated_recv.at[c, index],
            device_id=(me, target),
            device_id_type=pl.DeviceIdType.MESH,
        )

    def near_copy(c):
        return gated_copy(c, my_part, None, 0, near)

    def near_arrival(c):
        return gated_copy(c, near, None, 0, near)

    def far_copy(c, core):
        return pltpu.make_async_remote_copy(
            src_ref=gated_buf.at[c, my_part, core],
            dst_ref=gated_buf.at[c, my_part, core],
            send_sem=gated_send.at[c, 1 + core],
            recv_sem=gated_recv.at[c, 1 + my_core],
            device_id=(me, far + core),
            device_id_type=pl.DeviceIdType.MESH,
        )

    def far_arrival(c, core):
        return gated_copy(c, far + core, my_core, 1 + core, far + core)

    def pass_copy(c, core, half):
        return gated_copy(c, far + core, half, 3 + core, near)

    barrier = pltpu.get_barrier_semaphore()
    for step in range(1, dp_count):
        pl.semaphore_signal(
            barrier, inc=1, device_id=(peer(step), my_part), device_id_type=pl.DeviceIdType.MESH
        )
    for step in range(1, mp_count):
        pl.semaphore_signal(
            barrier, inc=1, device_id=(me, part(step)), device_id_type=pl.DeviceIdType.MESH
        )

    slot_first = [jnp.int32(0)] * dp_count
    my_count = jnp.int32(0)
    my_first = jnp.int32(0)
    my_history = jnp.int32(0)
    first = jnp.int32(0)
    for user in range(users):
        count = counts_ref[user]
        owner = owner_ref[user]
        slot_first = [
            jnp.where(owner == slot, first, slot_first[slot]) for slot in range(dp_count)
        ]
        mine = owner == me
        my_count = jnp.where(mine, count, my_count)
        my_first = jnp.where(mine, first, my_first)
        my_history = jnp.where(mine, history_ref[user], my_history)
        first = first + count
    slot_row = [
        lax.div(value - me + (dp_count - 1), dp_count) - (0 if slot in large else low * TILE)
        for slot, value in enumerate(slot_first)
    ]
    first_step = jnp.where(is_large, 0, low)

    row_id = lax.broadcasted_iota(jnp.int32, (TILE, local_rows), 1)
    tile_id = lax.broadcasted_iota(jnp.int32, (TILE, local_rows), 0)
    offset = row_id - tile_id

    def pack(c, slots):
        picked = jnp.concatenate(
            [
                jnp.where(offset == slot_row[slot] + c * TILE, 1.0, 0.0).astype(jnp.bfloat16)
                for slot in slots
            ],
            axis=0,
        )
        sent = jnp.dot(picked, rows_ref[...], preferred_element_type=jnp.float32)
        return sent.astype(jnp.bfloat16).reshape(len(slots), TILE, 4 * width)

    def for_all(c):
        return jnp.logical_and(c >= low, c < high)

    def for_large(c):
        return jnp.logical_or(c < low, jnp.logical_and(c >= high, c < chunks))

    def pack_into(c):
        @pl.when(for_all(c))
        def _():
            send_buf[c] = pack(c, range(dp_count))

        if high - low < chunks:

            @pl.when(for_large(c))
            def _():
                sent = pack(c, large)
                for index, slot in enumerate(large):
                    send_buf[c, slot] = sent[index]

    def each_copy(c, act):
        @pl.when(for_all(c))
        def _():
            for step in range(1, dp_count):
                act(row_copy(c, me, peer(step)))

        if high - low < chunks:

            @pl.when(for_large(c))
            def _():
                for slot in large:

                    @pl.when(me != slot)
                    def _():
                        act(row_copy(c, me, slot))

    def post(c):
        each_copy(c, lambda copy: copy.start())

    pack_into(0)
    pl.semaphore_wait(barrier, dp_count - 1 + mp_count - 1)
    post(0)
    pack_into(1)
    post(1)
    pack_into(2)

    place = lax.broadcasted_iota(jnp.int32, (chunk, chunk), 0)
    landed = lax.broadcasted_iota(jnp.int32, (chunk, chunk), 1)
    source_of = landed // TILE
    ordered_at = dp_count * (landed - source_of * TILE) + lax.rem(
        source_of - lax.rem(my_first, dp_count) + dp_count, dp_count
    )
    perm_buf[...] = jnp.where(place == ordered_at, 1.0, 0.0).astype(jnp.bfloat16)
    keys_buf[...] = cache_ref[:, :width].astype(jnp.float32).T.astype(jnp.bfloat16)
    history_id = lax.broadcasted_iota(jnp.int32, (history_cap, width), 0)
    values_buf[...] = jnp.where(
        history_id < my_history, cache_ref[:, width:].astype(jnp.float32), 0.0
    ).astype(jnp.bfloat16)
    line = lax.broadcasted_iota(jnp.int32, (8, chunk), 0)
    chunk_row = lax.broadcasted_iota(jnp.int32, (chunk, 1), 0)
    inverse = 1.0 / (my_history + 1).astype(jnp.float32)

    def attend(c):
        recv_buf[c, me] = send_buf[c, me]
        for step in range(1, dp_count):
            row_copy(c, peer(step), me).wait_recv()
        arrived = recv_buf[c].reshape(chunk, 4 * width)
        ordered = jnp.dot(perm_buf[...], arrived, preferred_element_type=jnp.float32)
        here = pl.ds(pl.multiple_of((c - first_step) * chunk, chunk), chunk)
        live = (c - first_step) * chunk + chunk_row < my_count
        kv_ref[here, :] = jnp.where(live, ordered[:, width : 3 * width], 0.0).astype(jnp.bfloat16)
        gate_buf[...] = ordered[:, 3 * width :]
        total = jnp.zeros((chunk, DH), jnp.float32)
        squares = jnp.zeros((chunk, DH), jnp.float32)
        for head in range(heads):
            columns = slice(head * DH, (head + 1) * DH)
            query = ordered[:, columns]
            key = ordered[:, width + head * DH : width + (head + 1) * DH]
            value = ordered[:, 2 * width + head * DH : 2 * width + (head + 1) * DH]
            half = (
                jnp.dot(
                    query.astype(jnp.bfloat16),
                    keys_buf[columns, :],
                    preferred_element_type=jnp.float32,
                )
                * half_scale
            )
            summed = jnp.dot(
                half_silu(half).astype(jnp.bfloat16),
                values_buf[:, columns],
                preferred_element_type=jnp.float32,
            )
            own = jnp.sum(query * key, axis=1, keepdims=True) * half_scale
            attended = (summed + half_silu(own) * value) * inverse
            attended_buf[:, columns] = attended
            total = total + attended
            squares = squares + attended * attended
        total = jnp.sum(total.T, axis=0, keepdims=True)
        squares = jnp.sum(squares.T, axis=0, keepdims=True)
        stats_buf[c, my_part] = jnp.where(line == 0, total, jnp.where(line == 1, squares, 0.0))
        for step in range(1, mp_count):
            part_copy(stats_buf, stats_send, stats_recv, c, my_part, part(step)).start()

    def gate(c):
        for step in range(1, mp_count):
            part_copy(stats_buf, stats_send, stats_recv, c, part(step), my_part).wait_recv()
        stats = stats_buf[c, 0]
        for index in range(1, mp_count):
            stats = stats + stats_buf[c, index]
        mean = stats[0:1] / width_all
        variance = stats[1:2] / width_all - mean * mean
        stats = jnp.where(line == 0, mean, lax.rsqrt(variance + EPSILON))
        stats = jnp.concatenate([stats, jnp.zeros((128 - 8, chunk), jnp.float32)], axis=0).T
        normed = (attended_buf[...] - stats[:, 0:1]) * stats[:, 1:2]
        gated = (normed * gate_buf[...]).astype(jnp.bfloat16)
        gated_buf[c, my_part] = gated.reshape(2, chunk // 2, width)
        for core in range(2):
            far_copy(c, core).start()
        near_copy(c).start()

    def mix(c):
        def product(source):
            rows = pl.ds(pl.multiple_of(source * width, width), width)
            return jnp.dot(
                gated_buf[c, source].reshape(chunk, width),
                w_buf[rows, :],
                preferred_element_type=jnp.float32,
            )

        for core in range(2):
            far_arrival(c, core).wait_recv()
            pass_copy(c, core, my_core).start()
        mixed = product(my_part)
        near_arrival(c).wait_recv()
        mixed = mixed + product(near)
        for core in range(2):
            pass_copy(c, core, 1 - my_core).wait_recv()
            mixed = mixed + product(far + core)
        here = pl.ds(pl.multiple_of((c - first_step) * chunk, chunk), chunk)
        live = (c - first_step) * chunk + chunk_row < my_count
        out_ref[here, :] = jnp.where(live, mixed, 0.0).astype(jnp.bfloat16)

    def works(c):
        return jnp.logical_or(is_large, for_all(c))

    def step_of(c, carry):
        each_copy(c, lambda copy: copy.wait_send())
        post(c + 2)

        @pl.when(works(c))
        def _():
            attend(c)

        pack_into(c + 3)

        @pl.when(jnp.logical_and(c > 0, works(c - 1)))
        def _():
            mix(c - 1)

        @pl.when(works(c))
        def _():
            gate(c)

        return carry

    lax.fori_loop(0, 1, step_of, 0)
    fetch_w.wait()
    lax.fori_loop(1, chunks, step_of, 0)

    @pl.when(works(chunks - 1))
    def _():
        mix(chunks - 1)

    if high - low < chunks:
        rest = chunks - (high - low)

        @pl.when(jnp.logical_not(is_large))
        def _():
            kv_ref[(high - low) * chunk :, :] = jnp.zeros((rest * chunk, 2 * width), jnp.bfloat16)
            out_ref[(high - low) * chunk :, :] = jnp.zeros((rest * chunk, width), jnp.bfloat16)

    def finish_parts(c, carry):
        for step in range(1, mp_count):
            part_copy(stats_buf, stats_send, stats_recv, c, my_part, part(step)).wait_send()
        near_copy(c).wait_send()
        for core in range(2):
            far_copy(c, core).wait_send()
            pass_copy(c, core, my_core).wait_send()
        return carry

    lax.fori_loop(low, high, finish_parts, 0)
    if high - low < chunks:

        @pl.when(is_large)
        def _():
            lax.fori_loop(0, low, finish_parts, 0)
            lax.fori_loop(high, chunks, finish_parts, 0)


def kernel_device(
    low, high, large, variant, new_rows, counts, history_len, user_owner, cache_kv, w_out
):
    dp_count = lax.axis_size("dp")
    mp_count = lax.axis_size("mp")
    width = w_out.shape[1]
    local_rows = new_rows.shape[0]
    history_cap = cache_kv.shape[1]
    chunks = CAP // (dp_count * TILE)
    chunk = dp_count * TILE
    smem = pl.BlockSpec(memory_space=pltpu.SMEM)
    vmem = pl.BlockSpec(memory_space=pltpu.VMEM)
    dma = pltpu.SemaphoreType.DMA
    key_value, results = pl.pallas_call(
        functools.partial(layer_kernel, dp_count, mp_count, low, high, large),
        out_shape=(
            jax.ShapeDtypeStruct((CAP, 2 * width), jnp.bfloat16),
            jax.ShapeDtypeStruct((CAP, width), jnp.bfloat16),
        ),
        in_specs=[smem, smem, smem, vmem, vmem, pl.BlockSpec(memory_space=pltpu.HBM)],
        out_specs=(vmem, vmem),
        scratch_shapes=[
            pltpu.VMEM(w_out.shape, jnp.bfloat16),
            pltpu.VMEM((chunks, dp_count, TILE, 4 * width), jnp.bfloat16),
            pltpu.VMEM((chunks, dp_count, TILE, 4 * width), jnp.bfloat16),
            pltpu.VMEM((width, history_cap), jnp.bfloat16),
            pltpu.VMEM((history_cap, width), jnp.bfloat16),
            pltpu.VMEM((chunk, chunk), jnp.bfloat16),
            pltpu.VMEM((chunk, width), jnp.float32),
            pltpu.VMEM((chunk, width), jnp.float32),
            pltpu.VMEM((chunks, mp_count, 8, chunk), jnp.float32),
            pltpu.VMEM((chunks, mp_count, 2, chunk // 2, width), jnp.bfloat16),
            dma((chunks, dp_count)),
            dma((chunks, dp_count)),
            dma((chunks, mp_count)),
            dma((chunks, mp_count)),
            dma((chunks, 5)),
            dma((chunks, 5)),
            dma,
        ],
        compiler_params=pltpu.CompilerParams(
            collective_id=variant, has_side_effects=True, vmem_limit_bytes=40 * 2**20
        ),
    )(
        counts,
        history_len,
        user_owner,
        new_rows.reshape(local_rows, 4 * width),
        cache_kv.reshape(history_cap, 2 * width),
        w_out,
    )
    return (key_value.reshape(1, CAP, 2, width), results[None])


def choice_kernel(pairs, half, limit, counts_ref, owner_ref, choice_ref):
    fits = [jnp.bool_(True)] * len(pairs)
    for user in range(counts_ref.shape[0]):
        small = counts_ref[user] <= limit
        place = lax.rem(owner_ref[user], half)
        held = [jnp.logical_or(small, place == index) for index in range(half)]
        fits = [
            jnp.logical_and(fit, jnp.logical_or(held[a], held[b]))
            for fit, (a, b) in zip(fits, pairs)
        ]
    choice = jnp.int32(len(pairs))
    for variant, fit in enumerate(fits):
        choice = jnp.where(fit, jnp.int32(variant), choice)
    choice_ref[0] = choice


def switched_device(new_rows, counts, history_len, user_owner, cache_kv, w_out):
    dp_count = lax.axis_size("dp")
    chunks = CAP // (dp_count * TILE)
    half = dp_count // 2
    low, high = 1, 4
    pairs = list(itertools.combinations(range(half), 2))
    branches = [
        functools.partial(kernel_device, low, high, (a, b, a + half, b + half), variant)
        for variant, (a, b) in enumerate(pairs)
    ]
    branches.append(
        functools.partial(kernel_device, 0, chunks, tuple(range(dp_count)), len(pairs))
    )
    smem = pl.BlockSpec(memory_space=pltpu.SMEM)
    choice = pl.pallas_call(
        functools.partial(choice_kernel, pairs, half, (high - low) * dp_count * TILE),
        out_shape=jax.ShapeDtypeStruct((1,), jnp.int32),
        in_specs=[smem, smem],
        out_specs=smem,
    )(counts, user_owner)[0]
    return lax.switch(
        choice, branches, new_rows, counts, history_len, user_owner, cache_kv, w_out
    )


def solution(mesh):
    placed = (P(None, "dp", None, "mp"), P(), P(), P(), P("dp", None, None, "mp"), P(None, "mp"))
    fits = mesh.shape["dp"] * TILE == 128 and mesh.shape["mp"] == 4
    return jax.shard_map(
        switched_device if fits else general_device,
        mesh=mesh,
        in_specs=placed,
        out_specs=(P("dp", None, None, "mp"), P("dp", None, "mp")),
        check_vma=False,
    )
```

```python
import functools
import itertools
import math

import jax
import jax.numpy as jnp
from jax import lax
from jax.experimental import pallas as pl
from jax.experimental.pallas import tpu as pltpu
from jax.sharding import PartitionSpec as P

DH = 128
CAP = 640
TILE = 16


EPSILON = 1e-06


def normalize(attended, gate_rows, width_all):
    total_sum, total_squares = lax.psum(
        (jnp.sum(attended, axis=-1), jnp.sum(attended * attended, axis=-1)), "mp"
    )
    row_mean = total_sum / width_all
    row_var = total_squares / width_all - row_mean * row_mean
    normed = (attended - row_mean[:, None]) * lax.rsqrt(row_var + EPSILON)[:, None]
    return (normed * gate_rows.astype(jnp.float32)).astype(jnp.bfloat16)


def project(gated, w_out):
    return jnp.dot(
        lax.all_gather(gated, "mp", axis=1, tiled=True), w_out, preferred_element_type=jnp.float32
    )


def general_device(new_rows, counts, history_len, user_owner, cache_kv, w_out):
    dp_count = lax.axis_size("dp")
    my_index = lax.axis_index("dp")
    local_rows = new_rows.shape[0]
    per_peer = CAP // dp_count
    width_all = w_out.shape[0]
    user_ids = jnp.arange(counts.shape[0], dtype=jnp.int32)
    starts = jnp.cumsum(counts) - counts
    event_ids = jnp.arange(local_rows, dtype=jnp.int32) * dp_count + my_index
    row_user = jnp.sum((starts[None, :] <= event_ids[:, None]).astype(jnp.int32), axis=1) - 1
    one_hot = (user_ids[None, :] == row_user[:, None]).astype(jnp.int32)
    row_first = jnp.sum(one_hot * starts[None, :], axis=1)
    row_owner = jnp.sum(one_hot * user_owner[None, :], axis=1)
    position = (event_ids - row_first) // dp_count * dp_count + row_owner
    is_mine = (user_owner == my_index).astype(jnp.int32)
    new_count = jnp.sum(counts * is_mine)
    first_row = jnp.sum(starts * is_mine)
    history = jnp.sum(history_len * is_mine)
    is_live = jnp.arange(CAP, dtype=jnp.int32) < new_count
    event_rows = new_rows[:, 0]
    feature_here = event_rows.shape[-1]
    heads_here = feature_here // DH
    history_cap = cache_kv.shape[1]
    cache_keys = cache_kv[0, :, 0].reshape(history_cap, heads_here, DH)
    cache_values = cache_kv[0, :, 1].reshape(history_cap, heads_here, DH)
    score_scale = 1.0 / math.sqrt(DH)
    buffer = jnp.zeros((CAP,) + event_rows.shape[1:], event_rows.dtype).at[position].set(event_rows)
    arrived = lax.all_to_all(
        buffer.reshape((per_peer, dp_count) + event_rows.shape[1:]),
        "dp",
        split_axis=1,
        concat_axis=1,
        tiled=True,
    )
    ordered = jnp.roll(arrived, -first_row, axis=1).reshape((CAP,) + arrived.shape[2:])
    queries = ordered[:, 0].reshape(CAP, heads_here, DH)
    own_keys = ordered[:, 1].reshape(CAP, heads_here, DH)
    own_values = ordered[:, 2].reshape(CAP, heads_here, DH)
    scores = (
        jnp.einsum("ehd,jhd->hej", queries, cache_keys, preferred_element_type=jnp.float32)
        * score_scale
    )
    visible = jnp.arange(history_cap, dtype=jnp.int32) < history
    weights = jnp.where(visible[None, None, :], jax.nn.silu(scores), 0.0).astype(jnp.bfloat16)
    summed = jnp.einsum("hej,jhd->ehd", weights, cache_values, preferred_element_type=jnp.float32)
    own_score = (
        jnp.sum(queries.astype(jnp.float32) * own_keys.astype(jnp.float32), axis=-1) * score_scale
    )
    attended = (summed + jax.nn.silu(own_score)[:, :, None] * own_values.astype(jnp.float32)) / (
        history + 1
    ).astype(jnp.float32)
    attended = attended.reshape(CAP, feature_here)
    gated = normalize(attended, ordered[:, 3], width_all)
    mixed_rows = project(gated, w_out)
    results = jnp.where(is_live[:, None], mixed_rows, 0.0).astype(jnp.bfloat16)
    key_value = ordered[:, 1:3]
    return (key_value[None], results[None])


def half_silu(half):
    return half + half * jnp.tanh(half)


def layer_kernel(
    dp_count,
    mp_count,
    low,
    high,
    large,
    counts_ref,
    history_ref,
    owner_ref,
    rows_ref,
    cache_ref,
    w_ref,
    kv_ref,
    out_ref,
    w_buf,
    send_buf,
    recv_buf,
    keys_buf,
    values_buf,
    perm_buf,
    attended_buf,
    gate_buf,
    stats_buf,
    gated_buf,
    row_send,
    row_recv,
    stats_send,
    stats_recv,
    gated_send,
    gated_recv,
    w_sem,
):
    fetch_w = pltpu.make_async_copy(w_ref, w_buf, w_sem)
    fetch_w.start()
    me = lax.axis_index("dp")
    my_part = lax.axis_index("mp")
    users = counts_ref.shape[0]
    local_rows = rows_ref.shape[0]
    width = w_ref.shape[1]
    width_all = w_ref.shape[0]
    heads = width // DH
    history_cap = cache_ref.shape[0]
    chunks = send_buf.shape[0]
    chunk = dp_count * TILE
    half_scale = 0.5 / math.sqrt(DH)
    is_large = functools.reduce(jnp.logical_or, [me == slot for slot in large])

    def peer(step):
        return lax.rem(me + step, dp_count)

    def part(step):
        return lax.rem(my_part + step, mp_count)

    def row_copy(c, source, target):
        return pltpu.make_async_remote_copy(
            src_ref=send_buf.at[c, target],
            dst_ref=recv_buf.at[c, source],
            send_sem=row_send.at[c, target],
            recv_sem=row_recv.at[c, source],
            device_id=(target, my_part),
            device_id_type=pl.DeviceIdType.MESH,
        )

    def part_copy(buf, send_sem, recv_sem, c, source, target):
        return pltpu.make_async_remote_copy(
            src_ref=buf.at[c, source],
            dst_ref=buf.at[c, source],
            send_sem=send_sem.at[c, target],
            recv_sem=recv_sem.at[c, source],
            device_id=(me, target),
            device_id_type=pl.DeviceIdType.MESH,
        )

    my_core = lax.rem(my_part, 2)
    near = my_part + 1 - 2 * my_core
    far = lax.rem(my_part - my_core + 2, mp_count)

    def gated_copy(c, source, half, index, target):
        block = gated_buf.at[c, source] if half is None else gated_buf.at[c, source, half]
        return pltpu.make_async_remote_copy(
            src_ref=block,
            dst_ref=block,
            send_sem=gated_send.at[c, index],
            recv_sem=gated_recv.at[c, index],
            device_id=(me, target),
            device_id_type=pl.DeviceIdType.MESH,
        )

    def near_copy(c):
        return gated_copy(c, my_part, None, 0, near)

    def near_arrival(c):
        return gated_copy(c, near, None, 0, near)

    def far_copy(c, core):
        return pltpu.make_async_remote_copy(
            src_ref=gated_buf.at[c, my_part, core],
            dst_ref=gated_buf.at[c, my_part, core],
            send_sem=gated_send.at[c, 1 + core],
            recv_sem=gated_recv.at[c, 1 + my_core],
            device_id=(me, far + core),
            device_id_type=pl.DeviceIdType.MESH,
        )

    def far_arrival(c, core):
        return gated_copy(c, far + core, my_core, 1 + core, far + core)

    def pass_copy(c, core, half):
        return gated_copy(c, far + core, half, 3 + core, near)

    barrier = pltpu.get_barrier_semaphore()
    for step in range(1, dp_count):
        pl.semaphore_signal(
            barrier, inc=1, device_id=(peer(step), my_part), device_id_type=pl.DeviceIdType.MESH
        )
    for step in range(1, mp_count):
        pl.semaphore_signal(
            barrier, inc=1, device_id=(me, part(step)), device_id_type=pl.DeviceIdType.MESH
        )

    slot_first = [jnp.int32(0)] * dp_count
    my_count = jnp.int32(0)
    my_first = jnp.int32(0)
    my_history = jnp.int32(0)
    first = jnp.int32(0)
    for user in range(users):
        count = counts_ref[user]
        owner = owner_ref[user]
        slot_first = [
            jnp.where(owner == slot, first, slot_first[slot]) for slot in range(dp_count)
        ]
        mine = owner == me
        my_count = jnp.where(mine, count, my_count)
        my_first = jnp.where(mine, first, my_first)
        my_history = jnp.where(mine, history_ref[user], my_history)
        first = first + count
    slot_row = [
        lax.div(value - me + (dp_count - 1), dp_count) - (0 if slot in large else low * TILE)
        for slot, value in enumerate(slot_first)
    ]
    first_step = jnp.where(is_large, 0, low)

    row_id = lax.broadcasted_iota(jnp.int32, (TILE, local_rows), 1)
    tile_id = lax.broadcasted_iota(jnp.int32, (TILE, local_rows), 0)
    offset = row_id - tile_id

    def pack(c, slots):
        picked = jnp.concatenate(
            [
                jnp.where(offset == slot_row[slot] + c * TILE, 1.0, 0.0).astype(jnp.bfloat16)
                for slot in slots
            ],
            axis=0,
        )
        sent = jnp.dot(picked, rows_ref[...], preferred_element_type=jnp.float32)
        return sent.astype(jnp.bfloat16).reshape(len(slots), TILE, 4 * width)

    def for_all(c):
        return jnp.logical_and(c >= low, c < high)

    def for_large(c):
        return jnp.logical_or(c < low, jnp.logical_and(c >= high, c < chunks))

    def pack_into(c):
        @pl.when(for_all(c))
        def _():
            send_buf[c] = pack(c, range(dp_count))

        if high - low < chunks:

            @pl.when(for_large(c))
            def _():
                sent = pack(c, large)
                for index, slot in enumerate(large):
                    send_buf[c, slot] = sent[index]

    def each_copy(c, act):
        @pl.when(for_all(c))
        def _():
            for step in range(1, dp_count):
                act(row_copy(c, me, peer(step)))

        if high - low < chunks:

            @pl.when(for_large(c))
            def _():
                for slot in large:

                    @pl.when(me != slot)
                    def _():
                        act(row_copy(c, me, slot))

    def post(c):
        each_copy(c, lambda copy: copy.start())

    pack_into(0)
    pl.semaphore_wait(barrier, dp_count - 1 + mp_count - 1)
    post(0)
    pack_into(1)
    post(1)
    pack_into(2)

    place = lax.broadcasted_iota(jnp.int32, (chunk, chunk), 0)
    landed = lax.broadcasted_iota(jnp.int32, (chunk, chunk), 1)
    source_of = landed // TILE
    ordered_at = dp_count * (landed - source_of * TILE) + lax.rem(
        source_of - lax.rem(my_first, dp_count) + dp_count, dp_count
    )
    perm_buf[...] = jnp.where(place == ordered_at, 1.0, 0.0).astype(jnp.bfloat16)
    keys_buf[...] = cache_ref[:, :width].astype(jnp.float32).T.astype(jnp.bfloat16)
    history_id = lax.broadcasted_iota(jnp.int32, (history_cap, width), 0)
    values_buf[...] = jnp.where(
        history_id < my_history, cache_ref[:, width:].astype(jnp.float32), 0.0
    ).astype(jnp.bfloat16)
    line = lax.broadcasted_iota(jnp.int32, (8, chunk), 0)
    chunk_row = lax.broadcasted_iota(jnp.int32, (chunk, 1), 0)
    inverse = 1.0 / (my_history + 1).astype(jnp.float32)

    def attend(c):
        recv_buf[c, me] = send_buf[c, me]
        for step in range(1, dp_count):
            row_copy(c, peer(step), me).wait_recv()
        arrived = recv_buf[c].reshape(chunk, 4 * width)
        ordered = jnp.dot(perm_buf[...], arrived, preferred_element_type=jnp.float32)
        here = pl.ds(pl.multiple_of((c - first_step) * chunk, chunk), chunk)
        live = (c - first_step) * chunk + chunk_row < my_count
        kv_ref[here, :] = jnp.where(live, ordered[:, width : 3 * width], 0.0).astype(jnp.bfloat16)
        gate_buf[...] = ordered[:, 3 * width :]
        total = jnp.zeros((chunk, DH), jnp.float32)
        squares = jnp.zeros((chunk, DH), jnp.float32)
        for head in range(heads):
            columns = slice(head * DH, (head + 1) * DH)
            query = ordered[:, columns]
            key = ordered[:, width + head * DH : width + (head + 1) * DH]
            value = ordered[:, 2 * width + head * DH : 2 * width + (head + 1) * DH]
            half = (
                jnp.dot(
                    query.astype(jnp.bfloat16),
                    keys_buf[columns, :],
                    preferred_element_type=jnp.float32,
                )
                * half_scale
            )
            summed = jnp.dot(
                half_silu(half).astype(jnp.bfloat16),
                values_buf[:, columns],
                preferred_element_type=jnp.float32,
            )
            own = jnp.sum(query * key, axis=1, keepdims=True) * half_scale
            attended = (summed + half_silu(own) * value) * inverse
            attended_buf[:, columns] = attended
            total = total + attended
            squares = squares + attended * attended
        total = jnp.sum(total.T, axis=0, keepdims=True)
        squares = jnp.sum(squares.T, axis=0, keepdims=True)
        stats_buf[c, my_part] = jnp.where(line == 0, total, jnp.where(line == 1, squares, 0.0))
        for step in range(1, mp_count):
            part_copy(stats_buf, stats_send, stats_recv, c, my_part, part(step)).start()

    def gate(c):
        for step in range(1, mp_count):
            part_copy(stats_buf, stats_send, stats_recv, c, part(step), my_part).wait_recv()
        stats = stats_buf[c, 0]
        for index in range(1, mp_count):
            stats = stats + stats_buf[c, index]
        mean = stats[0:1] / width_all
        variance = stats[1:2] / width_all - mean * mean
        stats = jnp.where(line == 0, mean, lax.rsqrt(variance + EPSILON))
        stats = jnp.concatenate([stats, jnp.zeros((128 - 8, chunk), jnp.float32)], axis=0).T
        normed = (attended_buf[...] - stats[:, 0:1]) * stats[:, 1:2]
        gated = (normed * gate_buf[...]).astype(jnp.bfloat16)
        gated_buf[c, my_part] = gated.reshape(2, chunk // 2, width)
        for core in range(2):
            far_copy(c, core).start()
        near_copy(c).start()

    def mix(c):
        def product(source):
            rows = pl.ds(pl.multiple_of(source * width, width), width)
            return jnp.dot(
                gated_buf[c, source].reshape(chunk, width),
                w_buf[rows, :],
                preferred_element_type=jnp.float32,
            )

        for core in range(2):
            far_arrival(c, core).wait_recv()
            pass_copy(c, core, my_core).start()
        mixed = product(my_part)
        near_arrival(c).wait_recv()
        mixed = mixed + product(near)
        for core in range(2):
            pass_copy(c, core, 1 - my_core).wait_recv()
            mixed = mixed + product(far + core)
        here = pl.ds(pl.multiple_of((c - first_step) * chunk, chunk), chunk)
        live = (c - first_step) * chunk + chunk_row < my_count
        out_ref[here, :] = jnp.where(live, mixed, 0.0).astype(jnp.bfloat16)

    def works(c):
        return jnp.logical_or(is_large, for_all(c))

    def step_of(c, carry):
        each_copy(c, lambda copy: copy.wait_send())
        post(c + 2)

        @pl.when(works(c))
        def _():
            attend(c)

        pack_into(c + 3)

        @pl.when(jnp.logical_and(c > 0, works(c - 1)))
        def _():
            mix(c - 1)

        @pl.when(works(c))
        def _():
            gate(c)

        return carry

    lax.fori_loop(0, 1, step_of, 0)
    fetch_w.wait()
    lax.fori_loop(1, chunks, step_of, 0)

    @pl.when(works(chunks - 1))
    def _():
        mix(chunks - 1)

    if high - low < chunks:
        rest = chunks - (high - low)

        @pl.when(jnp.logical_not(is_large))
        def _():
            kv_ref[(high - low) * chunk :, :] = jnp.zeros((rest * chunk, 2 * width), jnp.bfloat16)
            out_ref[(high - low) * chunk :, :] = jnp.zeros((rest * chunk, width), jnp.bfloat16)

    def finish_parts(c, carry):
        for step in range(1, mp_count):
            part_copy(stats_buf, stats_send, stats_recv, c, my_part, part(step)).wait_send()
        near_copy(c).wait_send()
        for core in range(2):
            far_copy(c, core).wait_send()
            pass_copy(c, core, my_core).wait_send()
        return carry

    lax.fori_loop(low, high, finish_parts, 0)
    if high - low < chunks:

        @pl.when(is_large)
        def _():
            lax.fori_loop(0, low, finish_parts, 0)
            lax.fori_loop(high, chunks, finish_parts, 0)


def kernel_device(
    low, high, large, variant, new_rows, counts, history_len, user_owner, cache_kv, w_out
):
    dp_count = lax.axis_size("dp")
    mp_count = lax.axis_size("mp")
    width = w_out.shape[1]
    local_rows = new_rows.shape[0]
    history_cap = cache_kv.shape[1]
    chunks = CAP // (dp_count * TILE)
    chunk = dp_count * TILE
    smem = pl.BlockSpec(memory_space=pltpu.SMEM)
    vmem = pl.BlockSpec(memory_space=pltpu.VMEM)
    dma = pltpu.SemaphoreType.DMA
    key_value, results = pl.pallas_call(
        functools.partial(layer_kernel, dp_count, mp_count, low, high, large),
        out_shape=(
            jax.ShapeDtypeStruct((CAP, 2 * width), jnp.bfloat16),
            jax.ShapeDtypeStruct((CAP, width), jnp.bfloat16),
        ),
        in_specs=[smem, smem, smem, vmem, vmem, pl.BlockSpec(memory_space=pltpu.HBM)],
        out_specs=(vmem, vmem),
        scratch_shapes=[
            pltpu.VMEM(w_out.shape, jnp.bfloat16),
            pltpu.VMEM((chunks, dp_count, TILE, 4 * width), jnp.bfloat16),
            pltpu.VMEM((chunks, dp_count, TILE, 4 * width), jnp.bfloat16),
            pltpu.VMEM((width, history_cap), jnp.bfloat16),
            pltpu.VMEM((history_cap, width), jnp.bfloat16),
            pltpu.VMEM((chunk, chunk), jnp.bfloat16),
            pltpu.VMEM((chunk, width), jnp.float32),
            pltpu.VMEM((chunk, width), jnp.float32),
            pltpu.VMEM((chunks, mp_count, 8, chunk), jnp.float32),
            pltpu.VMEM((chunks, mp_count, 2, chunk // 2, width), jnp.bfloat16),
            dma((chunks, dp_count)),
            dma((chunks, dp_count)),
            dma((chunks, mp_count)),
            dma((chunks, mp_count)),
            dma((chunks, 5)),
            dma((chunks, 5)),
            dma,
        ],
        compiler_params=pltpu.CompilerParams(
            collective_id=variant, has_side_effects=True, vmem_limit_bytes=40 * 2**20
        ),
    )(
        counts,
        history_len,
        user_owner,
        new_rows.reshape(local_rows, 4 * width),
        cache_kv.reshape(history_cap, 2 * width),
        w_out,
    )
    return (key_value.reshape(1, CAP, 2, width), results[None])


def choice_kernel(pairs, half, limits, counts_ref, owner_ref, choice_ref):
    fits = [[jnp.bool_(True)] * len(pairs) for _ in limits]
    for user in range(counts_ref.shape[0]):
        place = lax.rem(owner_ref[user], half)
        for level, limit in enumerate(limits):
            small = counts_ref[user] <= limit
            held = [jnp.logical_or(small, place == index) for index in range(half)]
            fits[level] = [
                jnp.logical_and(fit, jnp.logical_or(held[a], held[b]))
                for fit, (a, b) in zip(fits[level], pairs)
            ]
    choice = jnp.int32(len(limits) * len(pairs))
    for level in reversed(range(len(limits))):
        for index, fit in enumerate(fits[level]):
            choice = jnp.where(fit, jnp.int32(level * len(pairs) + index), choice)
    choice_ref[0] = choice


def switched_device(new_rows, counts, history_len, user_owner, cache_kv, w_out):
    dp_count = lax.axis_size("dp")
    chunks = CAP // (dp_count * TILE)
    half = dp_count // 2
    small_chunks = (2, 3)
    pairs = list(itertools.combinations(range(half), 2))
    kinds = [
        (chunks - held, (a, b, a + half, b + half)) for held in small_chunks for a, b in pairs
    ]
    kinds.append((0, tuple(range(dp_count))))
    branches = [
        functools.partial(kernel_device, low, chunks, large, variant)
        for variant, (low, large) in enumerate(kinds)
    ]
    limits = [held * dp_count * TILE for held in small_chunks]
    smem = pl.BlockSpec(memory_space=pltpu.SMEM)
    choice = pl.pallas_call(
        functools.partial(choice_kernel, pairs, half, limits),
        out_shape=jax.ShapeDtypeStruct((1,), jnp.int32),
        in_specs=[smem, smem],
        out_specs=smem,
    )(counts, user_owner)[0]
    return lax.switch(
        choice, branches, new_rows, counts, history_len, user_owner, cache_kv, w_out
    )


def solution(mesh):
    placed = (P(None, "dp", None, "mp"), P(), P(), P(), P("dp", None, None, "mp"), P(None, "mp"))
    fits = mesh.shape["dp"] * TILE == 128 and mesh.shape["mp"] == 4
    return jax.shard_map(
        switched_device if fits else general_device,
        mesh=mesh,
        in_specs=placed,
        out_specs=(P("dp", None, None, "mp"), P("dp", None, "mp")),
        check_vma=False,
    )
```

```python
import functools
import itertools
import math

import jax
import jax.numpy as jnp
from jax import lax
from jax.experimental import pallas as pl
from jax.experimental.pallas import tpu as pltpu
from jax.sharding import PartitionSpec as P

DH = 128
CAP = 640
TILE = 16


EPSILON = 1e-06


def normalize(attended, gate_rows, width_all):
    total_sum, total_squares = lax.psum(
        (jnp.sum(attended, axis=-1), jnp.sum(attended * attended, axis=-1)), "mp"
    )
    row_mean = total_sum / width_all
    row_var = total_squares / width_all - row_mean * row_mean
    normed = (attended - row_mean[:, None]) * lax.rsqrt(row_var + EPSILON)[:, None]
    return (normed * gate_rows.astype(jnp.float32)).astype(jnp.bfloat16)


def project(gated, w_out):
    return jnp.dot(
        lax.all_gather(gated, "mp", axis=1, tiled=True), w_out, preferred_element_type=jnp.float32
    )


def general_device(new_rows, counts, history_len, user_owner, cache_kv, w_out):
    dp_count = lax.axis_size("dp")
    my_index = lax.axis_index("dp")
    local_rows = new_rows.shape[0]
    per_peer = CAP // dp_count
    width_all = w_out.shape[0]
    user_ids = jnp.arange(counts.shape[0], dtype=jnp.int32)
    starts = jnp.cumsum(counts) - counts
    event_ids = jnp.arange(local_rows, dtype=jnp.int32) * dp_count + my_index
    row_user = jnp.sum((starts[None, :] <= event_ids[:, None]).astype(jnp.int32), axis=1) - 1
    one_hot = (user_ids[None, :] == row_user[:, None]).astype(jnp.int32)
    row_first = jnp.sum(one_hot * starts[None, :], axis=1)
    row_owner = jnp.sum(one_hot * user_owner[None, :], axis=1)
    position = (event_ids - row_first) // dp_count * dp_count + row_owner
    is_mine = (user_owner == my_index).astype(jnp.int32)
    new_count = jnp.sum(counts * is_mine)
    first_row = jnp.sum(starts * is_mine)
    history = jnp.sum(history_len * is_mine)
    is_live = jnp.arange(CAP, dtype=jnp.int32) < new_count
    event_rows = new_rows[:, 0]
    feature_here = event_rows.shape[-1]
    heads_here = feature_here // DH
    history_cap = cache_kv.shape[1]
    cache_keys = cache_kv[0, :, 0].reshape(history_cap, heads_here, DH)
    cache_values = cache_kv[0, :, 1].reshape(history_cap, heads_here, DH)
    score_scale = 1.0 / math.sqrt(DH)
    buffer = jnp.zeros((CAP,) + event_rows.shape[1:], event_rows.dtype).at[position].set(event_rows)
    arrived = lax.all_to_all(
        buffer.reshape((per_peer, dp_count) + event_rows.shape[1:]),
        "dp",
        split_axis=1,
        concat_axis=1,
        tiled=True,
    )
    ordered = jnp.roll(arrived, -first_row, axis=1).reshape((CAP,) + arrived.shape[2:])
    queries = ordered[:, 0].reshape(CAP, heads_here, DH)
    own_keys = ordered[:, 1].reshape(CAP, heads_here, DH)
    own_values = ordered[:, 2].reshape(CAP, heads_here, DH)
    scores = (
        jnp.einsum("ehd,jhd->hej", queries, cache_keys, preferred_element_type=jnp.float32)
        * score_scale
    )
    visible = jnp.arange(history_cap, dtype=jnp.int32) < history
    weights = jnp.where(visible[None, None, :], jax.nn.silu(scores), 0.0).astype(jnp.bfloat16)
    summed = jnp.einsum("hej,jhd->ehd", weights, cache_values, preferred_element_type=jnp.float32)
    own_score = (
        jnp.sum(queries.astype(jnp.float32) * own_keys.astype(jnp.float32), axis=-1) * score_scale
    )
    attended = (summed + jax.nn.silu(own_score)[:, :, None] * own_values.astype(jnp.float32)) / (
        history + 1
    ).astype(jnp.float32)
    attended = attended.reshape(CAP, feature_here)
    gated = normalize(attended, ordered[:, 3], width_all)
    mixed_rows = project(gated, w_out)
    results = jnp.where(is_live[:, None], mixed_rows, 0.0).astype(jnp.bfloat16)
    key_value = ordered[:, 1:3]
    return (key_value[None], results[None])


def half_silu(half):
    return half + half * jnp.tanh(half)


def layer_kernel(
    dp_count,
    mp_count,
    low,
    high,
    large,
    counts_ref,
    history_ref,
    owner_ref,
    rows_ref,
    cache_ref,
    w_ref,
    kv_ref,
    out_ref,
    w_buf,
    send_buf,
    recv_buf,
    keys_buf,
    values_buf,
    perm_buf,
    attended_buf,
    gate_buf,
    stats_buf,
    gated_buf,
    row_send,
    row_recv,
    stats_send,
    stats_recv,
    gated_send,
    gated_recv,
    w_sem,
):
    fetch_w = pltpu.make_async_copy(w_ref, w_buf, w_sem)
    fetch_w.start()
    me = lax.axis_index("dp")
    my_part = lax.axis_index("mp")
    users = counts_ref.shape[0]
    local_rows = rows_ref.shape[0]
    width = w_ref.shape[1]
    width_all = w_ref.shape[0]
    heads = width // DH
    history_cap = cache_ref.shape[0]
    chunks = send_buf.shape[0]
    chunk = dp_count * TILE
    half_scale = 0.5 / math.sqrt(DH)
    is_large = functools.reduce(jnp.logical_or, [me == slot for slot in large])

    def peer(step):
        return lax.rem(me + step, dp_count)

    def part(step):
        return lax.rem(my_part + step, mp_count)

    def row_copy(c, source, target):
        return pltpu.make_async_remote_copy(
            src_ref=send_buf.at[c, target],
            dst_ref=recv_buf.at[c, source],
            send_sem=row_send.at[c, target],
            recv_sem=row_recv.at[c, source],
            device_id=(target, my_part),
            device_id_type=pl.DeviceIdType.MESH,
        )

    def part_copy(buf, send_sem, recv_sem, c, source, target):
        return pltpu.make_async_remote_copy(
            src_ref=buf.at[c, source],
            dst_ref=buf.at[c, source],
            send_sem=send_sem.at[c, target],
            recv_sem=recv_sem.at[c, source],
            device_id=(me, target),
            device_id_type=pl.DeviceIdType.MESH,
        )

    my_core = lax.rem(my_part, 2)
    near = my_part + 1 - 2 * my_core
    far = lax.rem(my_part - my_core + 2, mp_count)

    def gated_copy(c, source, half, index, target):
        block = gated_buf.at[c, source] if half is None else gated_buf.at[c, source, half]
        return pltpu.make_async_remote_copy(
            src_ref=block,
            dst_ref=block,
            send_sem=gated_send.at[c, index],
            recv_sem=gated_recv.at[c, index],
            device_id=(me, target),
            device_id_type=pl.DeviceIdType.MESH,
        )

    def near_copy(c):
        return gated_copy(c, my_part, None, 0, near)

    def near_arrival(c):
        return gated_copy(c, near, None, 0, near)

    def far_copy(c, core):
        return pltpu.make_async_remote_copy(
            src_ref=gated_buf.at[c, my_part, core],
            dst_ref=gated_buf.at[c, my_part, core],
            send_sem=gated_send.at[c, 1 + core],
            recv_sem=gated_recv.at[c, 1 + my_core],
            device_id=(me, far + core),
            device_id_type=pl.DeviceIdType.MESH,
        )

    def far_arrival(c, core):
        return gated_copy(c, far + core, my_core, 1 + core, far + core)

    def pass_copy(c, core, half):
        return gated_copy(c, far + core, half, 3 + core, near)

    barrier = pltpu.get_barrier_semaphore()
    for step in range(1, dp_count):
        pl.semaphore_signal(
            barrier, inc=1, device_id=(peer(step), my_part), device_id_type=pl.DeviceIdType.MESH
        )
    for step in range(1, mp_count):
        pl.semaphore_signal(
            barrier, inc=1, device_id=(me, part(step)), device_id_type=pl.DeviceIdType.MESH
        )

    slot_first = [jnp.int32(0)] * dp_count
    my_count = jnp.int32(0)
    my_first = jnp.int32(0)
    my_history = jnp.int32(0)
    first = jnp.int32(0)
    for user in range(users):
        count = counts_ref[user]
        owner = owner_ref[user]
        slot_first = [
            jnp.where(owner == slot, first, slot_first[slot]) for slot in range(dp_count)
        ]
        mine = owner == me
        my_count = jnp.where(mine, count, my_count)
        my_first = jnp.where(mine, first, my_first)
        my_history = jnp.where(mine, history_ref[user], my_history)
        first = first + count
    slot_row = [
        lax.div(value - me + (dp_count - 1), dp_count) - (0 if slot in large else low * TILE)
        for slot, value in enumerate(slot_first)
    ]
    first_step = jnp.where(is_large, 0, low)

    row_id = lax.broadcasted_iota(jnp.int32, (TILE, local_rows), 1)
    tile_id = lax.broadcasted_iota(jnp.int32, (TILE, local_rows), 0)
    offset = row_id - tile_id

    def pack(c, slots):
        picked = jnp.concatenate(
            [
                jnp.where(offset == slot_row[slot] + c * TILE, 1.0, 0.0).astype(jnp.bfloat16)
                for slot in slots
            ],
            axis=0,
        )
        sent = jnp.dot(picked, rows_ref[...], preferred_element_type=jnp.float32)
        return sent.astype(jnp.bfloat16).reshape(len(slots), TILE, 4 * width)

    def for_all(c):
        return jnp.logical_and(c >= low, c < high)

    def for_large(c):
        return jnp.logical_or(c < low, jnp.logical_and(c >= high, c < chunks))

    def pack_into(c):
        @pl.when(for_all(c))
        def _():
            send_buf[c] = pack(c, range(dp_count))

        if high - low < chunks:

            @pl.when(for_large(c))
            def _():
                sent = pack(c, large)
                for index, slot in enumerate(large):
                    send_buf[c, slot] = sent[index]

    def each_copy(c, act):
        @pl.when(for_all(c))
        def _():
            for step in range(1, dp_count):
                act(row_copy(c, me, peer(step)))

        if high - low < chunks:

            @pl.when(for_large(c))
            def _():
                for slot in large:

                    @pl.when(me != slot)
                    def _():
                        act(row_copy(c, me, slot))

    def post(c):
        each_copy(c, lambda copy: copy.start())

    pack_into(0)
    pl.semaphore_wait(barrier, dp_count - 1 + mp_count - 1)
    post(0)
    pack_into(1)
    post(1)
    pack_into(2)

    place = lax.broadcasted_iota(jnp.int32, (chunk, chunk), 0)
    landed = lax.broadcasted_iota(jnp.int32, (chunk, chunk), 1)
    source_of = landed // TILE
    ordered_at = dp_count * (landed - source_of * TILE) + lax.rem(
        source_of - lax.rem(my_first, dp_count) + dp_count, dp_count
    )
    perm_buf[...] = jnp.where(place == ordered_at, 1.0, 0.0).astype(jnp.bfloat16)
    keys_buf[...] = cache_ref[:, :width].astype(jnp.float32).T.astype(jnp.bfloat16)
    history_id = lax.broadcasted_iota(jnp.int32, (history_cap, width), 0)
    values_buf[...] = jnp.where(
        history_id < my_history, cache_ref[:, width:].astype(jnp.float32), 0.0
    ).astype(jnp.bfloat16)
    line = lax.broadcasted_iota(jnp.int32, (8, chunk), 0)
    chunk_row = lax.broadcasted_iota(jnp.int32, (chunk, 1), 0)
    inverse = 1.0 / (my_history + 1).astype(jnp.float32)

    def attend(c):
        recv_buf[c, me] = send_buf[c, me]
        for step in range(1, dp_count):
            row_copy(c, peer(step), me).wait_recv()
        arrived = recv_buf[c].reshape(chunk, 4 * width)
        ordered = jnp.dot(perm_buf[...], arrived, preferred_element_type=jnp.float32)
        here = pl.ds(pl.multiple_of((c - first_step) * chunk, chunk), chunk)
        live = (c - first_step) * chunk + chunk_row < my_count
        kv_ref[here, :] = jnp.where(live, ordered[:, width : 3 * width], 0.0).astype(jnp.bfloat16)
        gate_buf[...] = ordered[:, 3 * width :]
        total = jnp.zeros((chunk, DH), jnp.float32)
        squares = jnp.zeros((chunk, DH), jnp.float32)
        for head in range(heads):
            columns = slice(head * DH, (head + 1) * DH)
            query = ordered[:, columns]
            key = ordered[:, width + head * DH : width + (head + 1) * DH]
            value = ordered[:, 2 * width + head * DH : 2 * width + (head + 1) * DH]
            half = (
                jnp.dot(
                    query.astype(jnp.bfloat16),
                    keys_buf[columns, :],
                    preferred_element_type=jnp.float32,
                )
                * half_scale
            )
            summed = jnp.dot(
                half_silu(half).astype(jnp.bfloat16),
                values_buf[:, columns],
                preferred_element_type=jnp.float32,
            )
            own = jnp.sum(query * key, axis=1, keepdims=True) * half_scale
            attended = (summed + half_silu(own) * value) * inverse
            attended_buf[:, columns] = attended
            total = total + attended
            squares = squares + attended * attended
        total = jnp.sum(total.T, axis=0, keepdims=True)
        squares = jnp.sum(squares.T, axis=0, keepdims=True)
        stats_buf[c, my_part] = jnp.where(line == 0, total, jnp.where(line == 1, squares, 0.0))
        for step in range(1, mp_count):
            part_copy(stats_buf, stats_send, stats_recv, c, my_part, part(step)).start()

    def gate(c):
        for step in range(1, mp_count):
            part_copy(stats_buf, stats_send, stats_recv, c, part(step), my_part).wait_recv()
        stats = stats_buf[c, 0]
        for index in range(1, mp_count):
            stats = stats + stats_buf[c, index]
        mean = stats[0:1] / width_all
        variance = stats[1:2] / width_all - mean * mean
        stats = jnp.where(line == 0, mean, lax.rsqrt(variance + EPSILON))
        stats = jnp.concatenate([stats, jnp.zeros((128 - 8, chunk), jnp.float32)], axis=0).T
        normed = (attended_buf[...] - stats[:, 0:1]) * stats[:, 1:2]
        gated = (normed * gate_buf[...]).astype(jnp.bfloat16)
        gated_buf[c, my_part] = gated.reshape(2, chunk // 2, width)
        for core in range(2):
            far_copy(c, core).start()
        near_copy(c).start()

    def mix(c):
        def product(source):
            rows = pl.ds(pl.multiple_of(source * width, width), width)
            return jnp.dot(
                gated_buf[c, source].reshape(chunk, width),
                w_buf[rows, :],
                preferred_element_type=jnp.float32,
            )

        for core in range(2):
            far_arrival(c, core).wait_recv()
            pass_copy(c, core, my_core).start()
        mixed = product(my_part)
        near_arrival(c).wait_recv()
        mixed = mixed + product(near)
        for core in range(2):
            pass_copy(c, core, 1 - my_core).wait_recv()
            mixed = mixed + product(far + core)
        here = pl.ds(pl.multiple_of((c - first_step) * chunk, chunk), chunk)
        live = (c - first_step) * chunk + chunk_row < my_count
        out_ref[here, :] = jnp.where(live, mixed, 0.0).astype(jnp.bfloat16)

    def works(c):
        return jnp.logical_or(is_large, for_all(c))

    def step_of(c, carry):
        each_copy(c, lambda copy: copy.wait_send())
        post(c + 2)

        @pl.when(works(c))
        def _():
            attend(c)

        pack_into(c + 3)

        @pl.when(jnp.logical_and(c > 0, works(c - 1)))
        def _():
            mix(c - 1)

        @pl.when(works(c))
        def _():
            gate(c)

        return carry

    lax.fori_loop(0, 1, step_of, 0)
    fetch_w.wait()
    lax.fori_loop(1, chunks, step_of, 0)

    @pl.when(works(chunks - 1))
    def _():
        mix(chunks - 1)

    if high - low < chunks:
        rest = chunks - (high - low)

        @pl.when(jnp.logical_not(is_large))
        def _():
            kv_ref[(high - low) * chunk :, :] = jnp.zeros((rest * chunk, 2 * width), jnp.bfloat16)
            out_ref[(high - low) * chunk :, :] = jnp.zeros((rest * chunk, width), jnp.bfloat16)

    def finish_parts(c, carry):
        for step in range(1, mp_count):
            part_copy(stats_buf, stats_send, stats_recv, c, my_part, part(step)).wait_send()
        near_copy(c).wait_send()
        for core in range(2):
            far_copy(c, core).wait_send()
            pass_copy(c, core, my_core).wait_send()
        return carry

    lax.fori_loop(low, high, finish_parts, 0)
    if high - low < chunks:

        @pl.when(is_large)
        def _():
            lax.fori_loop(0, low, finish_parts, 0)
            lax.fori_loop(high, chunks, finish_parts, 0)


def kernel_device(
    low, high, large, variant, new_rows, counts, history_len, user_owner, cache_kv, w_out
):
    dp_count = lax.axis_size("dp")
    mp_count = lax.axis_size("mp")
    width = w_out.shape[1]
    local_rows = new_rows.shape[0]
    history_cap = cache_kv.shape[1]
    chunks = CAP // (dp_count * TILE)
    chunk = dp_count * TILE
    smem = pl.BlockSpec(memory_space=pltpu.SMEM)
    vmem = pl.BlockSpec(memory_space=pltpu.VMEM)
    dma = pltpu.SemaphoreType.DMA
    key_value, results = pl.pallas_call(
        functools.partial(layer_kernel, dp_count, mp_count, low, high, large),
        out_shape=(
            jax.ShapeDtypeStruct((CAP, 2 * width), jnp.bfloat16),
            jax.ShapeDtypeStruct((CAP, width), jnp.bfloat16),
        ),
        in_specs=[smem, smem, smem, vmem, vmem, pl.BlockSpec(memory_space=pltpu.HBM)],
        out_specs=(vmem, vmem),
        scratch_shapes=[
            pltpu.VMEM(w_out.shape, jnp.bfloat16),
            pltpu.VMEM((chunks, dp_count, TILE, 4 * width), jnp.bfloat16),
            pltpu.VMEM((chunks, dp_count, TILE, 4 * width), jnp.bfloat16),
            pltpu.VMEM((width, history_cap), jnp.bfloat16),
            pltpu.VMEM((history_cap, width), jnp.bfloat16),
            pltpu.VMEM((chunk, chunk), jnp.bfloat16),
            pltpu.VMEM((chunk, width), jnp.float32),
            pltpu.VMEM((chunk, width), jnp.float32),
            pltpu.VMEM((chunks, mp_count, 8, chunk), jnp.float32),
            pltpu.VMEM((chunks, mp_count, 2, chunk // 2, width), jnp.bfloat16),
            dma((chunks, dp_count)),
            dma((chunks, dp_count)),
            dma((chunks, mp_count)),
            dma((chunks, mp_count)),
            dma((chunks, 5)),
            dma((chunks, 5)),
            dma,
        ],
        compiler_params=pltpu.CompilerParams(
            collective_id=variant, has_side_effects=True, vmem_limit_bytes=40 * 2**20
        ),
    )(
        counts,
        history_len,
        user_owner,
        new_rows.reshape(local_rows, 4 * width),
        cache_kv.reshape(history_cap, 2 * width),
        w_out,
    )
    return (key_value.reshape(1, CAP, 2, width), results[None])


def choice_kernel(pairs, half, limits, counts_ref, owner_ref, choice_ref):
    fits = [[jnp.bool_(True)] * len(pairs) for _ in limits]
    for user in range(counts_ref.shape[0]):
        place = lax.rem(owner_ref[user], half)
        for level, limit in enumerate(limits):
            small = counts_ref[user] <= limit
            held = [jnp.logical_or(small, place == index) for index in range(half)]
            fits[level] = [
                jnp.logical_and(fit, jnp.logical_or(held[a], held[b]))
                for fit, (a, b) in zip(fits[level], pairs)
            ]
    choice = jnp.int32(len(limits) * len(pairs))
    for level in reversed(range(len(limits))):
        for index, fit in enumerate(fits[level]):
            choice = jnp.where(fit, jnp.int32(level * len(pairs) + index), choice)
    choice_ref[0] = choice


def switched_device(new_rows, counts, history_len, user_owner, cache_kv, w_out):
    dp_count = lax.axis_size("dp")
    chunks = CAP // (dp_count * TILE)
    half = dp_count // 2
    small_chunks = (3,)
    pairs = list(itertools.combinations(range(half), 2))
    kinds = [
        (chunks - held, (a, b, a + half, b + half)) for held in small_chunks for a, b in pairs
    ]
    kinds.append((0, tuple(range(dp_count))))
    branches = [
        functools.partial(kernel_device, low, chunks, large, variant)
        for variant, (low, large) in enumerate(kinds)
    ]
    limits = [held * dp_count * TILE for held in small_chunks]
    smem = pl.BlockSpec(memory_space=pltpu.SMEM)
    choice = pl.pallas_call(
        functools.partial(choice_kernel, pairs, half, limits),
        out_shape=jax.ShapeDtypeStruct((1,), jnp.int32),
        in_specs=[smem, smem],
        out_specs=smem,
    )(counts, user_owner)[0]
    return lax.switch(
        choice, branches, new_rows, counts, history_len, user_owner, cache_kv, w_out
    )


def solution(mesh):
    placed = (P(None, "dp", None, "mp"), P(), P(), P(), P("dp", None, None, "mp"), P(None, "mp"))
    fits = mesh.shape["dp"] * TILE == 128 and mesh.shape["mp"] == 4
    return jax.shard_map(
        switched_device if fits else general_device,
        mesh=mesh,
        in_specs=placed,
        out_specs=(P("dp", None, None, "mp"), P("dp", None, "mp")),
        check_vma=False,
    )
```
